128 devices in a mesh: dp: 4 (over x), row: 16 (over z, y), col: 2 (over core).
Axes of the slice: x: 4, y: 4, z: 4, core: 2. Of those that a mesh axis runs over, the one named last changes fastest.
Arguments:
- tokens: bfloat16 [2048, 14336], P('dp', 'row'), may hold values from -6 to 6
- frozen: bfloat16 [14336, 12288], P('row', 'col')
- adapter_down: bfloat16 [14336, 128], P('row')
- adapter_up: bfloat16 [128, 12288], P(None, 'col'), may hold values from -1.21 to 1.21
- magnitude: float32 [8, 12288], P(None, 'col'), may hold values from 0.5 to 4
- grad_out: bfloat16 [2048, 12288], P('dp', 'col'), may hold values from -6 to 6
- tenant_lengths: int32 [32], replicated, may hold values from 1 to 256, 2048 in all
- tenant_adapter: int32 [32], replicated, may hold values from 0 to 7
Outputs:
- adapted: bfloat16 [2048, 12288], P('dp', 'col')
- input_grad: bfloat16 [2048, 14336], P('dp', 'row')
- grad_down: float32 [14336, 128], P('row')
- grad_up: float32 [128, 12288], P(None, 'col')
- grad_magnitude: float32 [8, 12288], P(None, 'col')
The draws below stay inside these ranges and needn't reach their ends.
Inputs may be any that keep to these rules, and one draw needn't show every extreme that they name: `tenant_lengths`: the lengths sum to 2048.
All inputs are finite; a program needn't handle non-finite values.
Results may differ from the reference program's by a relative error of at most 0.0075.
Values may be sent and summed in bfloat16 or wider, within the bound.
No kernel may reach another device: no remote copies, remote signals or barrier semaphores. Data moves between devices by JAX's collectives and lax.ppermute only.
A program may use at most 192 MiB of HBM per device.

```python
import math
import jax
import jax.numpy as jnp
import numpy as np
from jax import lax

K = 14336
N = 12288
R = 16
ADP = 8
TENANTS = 32
TOKENS = 2048
AR = 128


def adapter_pair(key):
    key_up, key_own, key_shared = jax.random.split(jax.random.fold_in(key, 101), 3)
    up_values = 0.2 * jax.random.truncated_normal(key_up, -6.0, 6.0, (AR, N), jnp.float32)
    own_part = jax.random.normal(key_own, (K, AR), jnp.float32)
    shared_part = jax.random.normal(key_shared, (K, ADP), jnp.float32)
    down_values = (own_part + jnp.repeat(shared_part, R, axis=1)) / jnp.sqrt(jnp.float32(2 * K))
    return (down_values, up_values)


def draw_adapter_down(key, part):
    down_values, up_values = adapter_pair(key)
    return down_values.astype(jnp.bfloat16)


def draw_adapter_up(key, part):
    down_values, up_values = adapter_pair(key)
    return up_values.astype(jnp.bfloat16)


def draw_frozen(key, part):
    down_values, up_values = adapter_pair(key)
    key = jax.random.fold_in(key, 11)
    key_rows = jax.random.fold_in(key, 0)
    key_cols = jax.random.fold_in(key, 1)
    key_body = jax.random.fold_in(key, 2)
    key_pick = jax.random.fold_in(key, 4)
    ramp = jnp.exp(jnp.log(3.0) * jnp.arange(K, dtype=jnp.float32) / K)
    row_scale = ramp * jnp.exp(jax.random.uniform(key_rows, (K,), jnp.float32, 0.0, jnp.log(10.0)))
    col_scale = jnp.exp(jax.random.uniform(key_cols, (N,), jnp.float32, 0.0, jnp.log(10.0)))
    values = jax.random.normal(key_body, (K, N), jnp.float32)
    overall = 0.12
    picked = jax.random.randint(key_pick, (N,), 0, AR)
    columns = jnp.arange(N, dtype=jnp.int32)
    along = up_values[picked, columns] / 0.2
    aligned = down_values[:, picked] * along[None, :]
    base_part = values * row_scale[:, None] * (overall / jnp.sqrt(jnp.float32(K)))
    result = (base_part + aligned) * col_scale[None, :]
    return result.astype(jnp.bfloat16)


def touch_ends(array, own_key, least, high):
    longest = array.shape.index(max(array.shape))
    spots = []
    for shift in (0, 1):
        where = [jax.random.randint(jax.random.fold_in(own_key, axis), (), 0, length) for axis, length in enumerate(array.shape)]
        where[longest] = (where[longest] + shift) % array.shape[longest]
        spots.append(tuple(where))
    return array.at[spots[0]].set(least).at[spots[1]].set(high)


def block_scale(own_key, extent, cuts, least, high):
    factor_of, own = 1.0, jax.random.fold_in(own_key, 6)
    for dim, shards_of in cuts:
        heights = jnp.exp(jax.random.uniform(jax.random.fold_in(own, dim), (shards_of,), jnp.float32, least / len(cuts), high / len(cuts)))
        factor_of = factor_of * jnp.repeat(heights, extent[dim] // shards_of).reshape([-1 if axis == dim else 1 for axis in range(len(extent))])
    return factor_of


def profile(count, total, bound, lean):
    loads = [(1 << 20) // math.isqrt(standing ** lean) + 1 for standing in range(2, count + 1)]
    spare, given = total - bound - (count - 1), [1] * (count - 1)
    while spare > 0:
        movable = [i for i in range(count - 1) if given[i] < bound]
        mass, remaining = sum([loads[i] for i in movable]), spare
        for i in movable:
            addition = min(bound - given[i], max(1, remaining * loads[i] // mass), spare)
            given[i] = given[i] + addition
            spare = spare - addition
    return np.array([bound] + given)


def ragged(key, number_of, total, limit, lean):
    if number_of == 2:
        one = jax.random.randint(key, (), max(1, total - limit), min(limit, total - 1) + 1)
        return jnp.stack([one, total - one])
    sizes = jnp.asarray(profile(number_of, total, limit, lean), jnp.int32)
    pairs = (number_of - 1) // 2
    source_of, sink = sizes[1:1 + 2 * pairs:2], sizes[2:2 + 2 * pairs:2]
    margin = jnp.minimum(source_of - 1, limit - sink)
    shifted = jax.random.randint(jax.random.fold_in(key, 1), (pairs,), 0, 1 << 20) % (margin + 1)
    sizes = sizes.at[1:1 + 2 * pairs:2].set(source_of - shifted).at[2:2 + 2 * pairs:2].set(sink + shifted)
    return sizes[jax.random.permutation(jax.random.fold_in(key, 2), number_of)]


def scatter_about(own_key, dims, width, reach, shards=(), kind=jnp.bfloat16):
    entries = jax.random.normal(own_key, dims, jnp.float32) * width
    if len(shards) > 0:
        entries = block_scale(own_key, dims, shards, -0.22, 0.18) * entries
    return jnp.clip(entries, min=-reach, max=reach).astype(kind)


def setup_inputs(seed: int = 0) -> dict:
    arg_keys = jax.random.split(jax.random.key(seed), 9)
    tokens = scatter_about(arg_keys[0], (TOKENS, K), 1.0, 6.0, ((0, 4), (1, 16)))
    frozen = draw_frozen(jax.random.fold_in(arg_keys[8], 71), 0)
    adapter_down = draw_adapter_down(jax.random.fold_in(arg_keys[8], 71), 0)
    adapter_up = draw_adapter_up(jax.random.fold_in(arg_keys[8], 71), 0)
    magnitude = jnp.clip(jnp.exp(math.log(4.0) - 2.0794415 * jax.random.uniform(arg_keys[4], (ADP, N), jnp.float32) ** block_scale(arg_keys[4], (ADP, N), ((1, 2),), -0.2, 0.2)), 0.5, 4.0)
    grad_out = scatter_about(arg_keys[5], (TOKENS, N), 1.0, 6.0, ((0, 4), (1, 2)))
    tenant_lengths = ragged(arg_keys[6], TENANTS, TOKENS, TOKENS // 8, 2).astype(jnp.int32)
    tenant_adapter = touch_ends(jax.random.randint(arg_keys[7], (TENANTS,), 0, ADP), jax.random.fold_in(arg_keys[7], 1), 0, ADP - 1).astype(jnp.int32)
    return {"tokens": tokens, "frozen": frozen, "adapter_down": adapter_down, "adapter_up": adapter_up, "magnitude": magnitude, "grad_out": grad_out, "tenant_lengths": tenant_lengths, "tenant_adapter": tenant_adapter}


def token_adapters(tenant_lengths, tenant_adapter, tok_count, first_token):
    starts_at = jnp.cumsum(tenant_lengths) - tenant_lengths
    position = first_token + jnp.arange(tok_count, dtype=jnp.int32)
    tenant = lax.optimization_barrier(jnp.sum((starts_at[None, :] <= position[:, None]).astype(jnp.int32), axis=1)) - 1
    picked = (tenant[:, None] == jnp.arange(tenant_lengths.shape[0], dtype=jnp.int32)[None, :]).astype(jnp.int32)
    return lax.optimization_barrier(jnp.sum(picked * tenant_adapter[None, :], axis=1))

def column_squares(squares, cross, gram, up_wide, rank_size, adapters):
    flat_cols = up_wide.shape[0]
    block_ids = jnp.arange(flat_cols, dtype=jnp.int32) // rank_size
    blocks = (block_ids[:, None] == block_ids[None, :]).astype(jnp.float32)
    gram_up = jnp.dot(gram * blocks, up_wide, precision=lax.Precision.HIGHEST)
    terms = (up_wide * (2.0 * cross + gram_up)).reshape(adapters, rank_size, -1)
    return squares[None, :] + lax.optimization_barrier(jnp.sum(terms, axis=1))

def reference(tokens, frozen, adapter_down, adapter_up, magnitude, grad_out, tenant_lengths, tenant_adapter):
    highest = lax.Precision.HIGHEST
    contract_first = (((0,), (0,)), ((), ()))
    contract_last = (((1,), (1,)), ((), ()))
    adapter = token_adapters(tenant_lengths, tenant_adapter, TOKENS, 0)
    one_hot = (adapter[:, None] == jnp.arange(ADP, dtype=jnp.int32)[None, :]).astype(jnp.float32)
    slot_mask = (adapter[:, None] == (jnp.arange(AR, dtype=jnp.int32) // R)[None, :]).astype(jnp.float32)
    squares = lax.optimization_barrier(jnp.sum(jnp.square(frozen.astype(jnp.float32)), axis=0))
    cross = lax.dot_general(adapter_down, frozen, contract_first, preferred_element_type=jnp.float32)
    gram = lax.dot_general(adapter_down, adapter_down, contract_first, preferred_element_type=jnp.float32)
    up_wide = adapter_up.astype(jnp.float32)
    col_sq = column_squares(squares, cross, gram, up_wide, R, ADP)
    col_norm = jnp.sqrt(col_sq + 1e-06)
    scale_table = magnitude / col_norm
    tok_scale = jnp.dot(one_hot, scale_table, precision=highest)
    down_full = jnp.dot(tokens, adapter_down, preferred_element_type=jnp.float32) * slot_mask
    mixed = jnp.dot(tokens, frozen, preferred_element_type=jnp.float32) + jnp.dot(down_full, up_wide, precision=highest)
    adapted = (tok_scale * mixed).astype(jnp.bfloat16)
    scaled_grad = (grad_out.astype(jnp.float32) * tok_scale).astype(jnp.bfloat16)
    back_full = lax.dot_general(scaled_grad, adapter_up, contract_last, preferred_element_type=jnp.float32) * slot_mask
    down_wide = adapter_down.astype(jnp.float32)
    input_grad = lax.dot_general(scaled_grad, frozen, contract_last, preferred_element_type=jnp.float32)
    input_grad = (input_grad + lax.dot_general(back_full, down_wide, contract_last, precision=highest)).astype(jnp.bfloat16)
    grad_down = lax.dot_general(tokens.astype(jnp.float32), back_full, contract_first, precision=highest)
    grad_up = lax.dot_general(down_full, scaled_grad.astype(jnp.float32), contract_first, precision=highest)
    mag_sum = lax.dot_general(one_hot, grad_out.astype(jnp.float32) * mixed, contract_first, precision=highest)
    return (adapted, input_grad, grad_down, grad_up, mag_sum / col_norm)
```

```python
import functools

import jax
import jax.numpy as jnp
from jax import lax
from jax.experimental import pallas as pl
from jax.experimental.pallas import tpu as pltpu
from jax.sharding import Mesh
from jax.sharding import PartitionSpec as P

BF = jnp.bfloat16
F32 = jnp.float32
SIDE = 4
PLAIN = (((1,), (0,)), ((), ()))
FIRST = (((0,), (0,)), ((), ()))
LAST = (((1,), (1,)), ((), ()))

STREAMS = (
    (("y", 1), ("y", 3), ("z", 1), ("z", 3)),
    (("y", 3), ("y", 1), ("z", 3), ("z", 1)),
    (("z", 1), ("z", 3), ("y", 1), ("y", 3)),
    (("z", 3), ("z", 1), ("y", 3), ("y", 1)),
)
SPAN = 512


def swap(values, pairing):
    axis, flip = pairing
    return lax.ppermute(values, axis, [(i, i ^ flip) for i in range(SIDE)])


def wide(values):
    return values.astype(F32)


def dot(a, b, dims=PLAIN):
    return lax.dot_general(a, b, dims, preferred_element_type=F32)


def split_parts(values):
    upper = values.astype(BF)
    return upper, (values - wide(upper)).astype(BF)


def token_adapters(tenant_lengths, tenant_adapter, tok_count, first_token):
    starts_at = jnp.cumsum(tenant_lengths) - tenant_lengths
    position = first_token + jnp.arange(tok_count, dtype=jnp.int32)
    tenant = jnp.sum((starts_at[None, :] <= position[:, None]).astype(jnp.int32), axis=1) - 1
    picked = (
        tenant[:, None] == jnp.arange(tenant_lengths.shape[0], dtype=jnp.int32)[None, :]
    ).astype(jnp.int32)
    return jnp.sum(picked * tenant_adapter[None, :], axis=1)


def squares_kernel(adapters, where, frozen, down, up, out):
    weights = frozen[...]
    maps = down[...]
    flat = maps.shape[1]
    rank = flat // adapters
    cross = dot(maps, weights, FIRST)
    gram = dot(maps, maps, FIRST)
    rows = lax.broadcasted_iota(jnp.int32, (flat, flat), 0) // rank
    cols = lax.broadcasted_iota(jnp.int32, (flat, flat), 1) // rank
    upper, lower = split_parts(jnp.where(rows == cols, gram, 0.0))
    outer = up[...]
    gram_up = dot(upper, outer) + dot(lower, outer)
    terms = wide(outer) * (2.0 * cross + gram_up)
    squares = jnp.sum(jnp.square(wide(weights)), axis=0, keepdims=True)
    out[...] = squares + jnp.sum(terms.reshape(adapters, rank, -1), axis=1)


def column_squares(frozen, down, up, adapters, quarter):
    depth, flat = down.shape
    steps = frozen.shape[1] // SIDE // SPAN
    return pl.pallas_call(
        functools.partial(squares_kernel, adapters),
        grid_spec=pltpu.PrefetchScalarGridSpec(
            num_scalar_prefetch=1,
            grid=(steps,),
            in_specs=[
                pl.BlockSpec((depth, SPAN), lambda j, at: (0, at[0] * steps + j)),
                pl.BlockSpec((depth, flat), lambda j, at: (0, 0)),
                pl.BlockSpec((flat, SPAN), lambda j, at: (0, at[0] * steps + j)),
            ],
            out_specs=pl.BlockSpec((adapters, SPAN), lambda j, at: (0, j)),
        ),
        out_shape=jax.ShapeDtypeStruct((adapters, steps * SPAN), F32),
        compiler_params=pltpu.CompilerParams(vmem_limit_bytes=32 << 20),
        name="squares",
    )(quarter[None], frozen, down, up)


def mixed_kernel(where, tok0, tok1, low0, low1, hot0, hot1, grad0, grad1, frozen, up, out, mag, left, hot):
    rows = tok0.shape[1]
    depth = tok0.shape[2]

    @pl.when(pl.program_id(0) == 0)
    def _():
        left[:rows, :depth] = tok0[0]
        left[rows:, :depth] = tok1[0]
        left[:rows, depth:] = low0[0]
        left[rows:, depth:] = low1[0]
        hot[:, :rows] = hot0[0]
        hot[:, rows:] = hot1[0]

    total = dot(left[:, :depth], frozen[...]) + dot(left[:, depth:], up[...])
    out[...] = total.astype(BF)
    grads = jnp.concatenate([grad0[0], grad1[0]], axis=0)
    mag[...] = dot(hot[...], (total * wide(grads)).astype(BF))[: mag.shape[0]]


def mixed_part(stream, blocks, tokens, low, hot, grads, frozen, up, adapters):
    _, rows, depth = tokens.shape
    flat = up.shape[0]
    width = frozen.shape[1] // len(STREAMS)
    steps = width // SPAN

    def pair(shape, moving):
        def at(which):
            return lambda j, at: (at[which], 0, stream * steps + j if moving else 0)

        return [pl.BlockSpec(shape, at(0)), pl.BlockSpec(shape, at(1))]

    return pl.pallas_call(
        mixed_kernel,
        grid_spec=pltpu.PrefetchScalarGridSpec(
            num_scalar_prefetch=1,
            grid=(steps,),
            in_specs=[
                *pair((1, rows, depth), False),
                *pair((1, rows, flat), False),
                *pair((1, hot.shape[1], rows), False),
                *pair((1, rows, SPAN), True),
                pl.BlockSpec((depth, SPAN), lambda j, at: (0, stream * steps + j)),
                pl.BlockSpec((flat, SPAN), lambda j, at: (0, stream * steps + j)),
            ],
            out_specs=[
                pl.BlockSpec((2 * rows, SPAN), lambda j, at: (0, j)),
                pl.BlockSpec((adapters, SPAN), lambda j, at: (0, j)),
            ],
            scratch_shapes=[
                pltpu.VMEM((2 * rows, depth + flat), BF),
                pltpu.VMEM((hot.shape[1], 2 * rows), BF),
            ],
        ),
        out_shape=[
            jax.ShapeDtypeStruct((2 * rows, width), BF),
            jax.ShapeDtypeStruct((adapters, width), F32),
        ],
        compiler_params=pltpu.CompilerParams(vmem_limit_bytes=32 << 20),
        cost_estimate=pl.CostEstimate(
            flops=4 * rows * (depth + flat) * width,
            bytes_accessed=2 * (depth + 5 * rows) * width,
            transcendentals=0,
        ),
        name="mixed",
    )(blocks, tokens, tokens, low, low, hot, hot, grads, grads, frozen, up)


def on_device(
    tokens, frozen, adapter_down, adapter_up, magnitude, grad_out, tenant_lengths, tenant_adapter
):
    tok_rows, depth = tokens.shape
    adapters, cols = magnitude.shape
    flat = adapter_down.shape[1]
    rank = flat // adapters
    block = tok_rows // SIDE
    width = cols // len(STREAMS)
    quarter = cols // SIDE
    place = {axis: lax.axis_index(axis) for axis in ("dp", "z", "y", "col")}

    adapter = token_adapters(tenant_lengths, tenant_adapter, tok_rows, place["dp"] * tok_rows)
    own = adapter[:, None] == jnp.arange(adapters, dtype=jnp.int32)[None, :]
    slots = adapter[:, None] == (jnp.arange(flat, dtype=jnp.int32) // rank)[None, :]

    sq_part = column_squares(frozen, adapter_down, adapter_up, adapters, place["dp"])
    down_part = jnp.where(slots, dot(tokens, adapter_down), 0.0)
    low = down_part.astype(BF)
    pieces = quarter // flat
    small = sq_part
    down_sum = down_part
    for step, pairing in enumerate((("y", 1), ("z", 1), ("y", 3), ("z", 3))):
        upper, lower = split_parts(small)
        parts = [down_sum.astype(BF)]
        for half in (upper, lower):
            parts += [half[:, i * flat : (i + 1) * flat] for i in range(pieces)]
        sent = jnp.concatenate(parts, axis=0)
        total = wide(sent) + wide(swap(sent, pairing))
        down_sum = total[:tok_rows]
        both = total[tok_rows:].reshape(2, pieces, adapters, flat)
        both = both[0] + both[1]
        small = jnp.concatenate([both[i] for i in range(pieces)], axis=1)
    col_sq = jnp.zeros((adapters, cols), F32)
    spots = (place["dp"], place["dp"] ^ 1, place["dp"] ^ 3, place["dp"] ^ 2)
    found = (
        small,
        swap(small, ("dp", 1)),
        swap(small, ("dp", 3)),
        swap(small, ("dp", 2)),
    )
    for spot, values in zip(spots, found, strict=True):
        col_sq = lax.dynamic_update_slice(col_sq, values, (0, spot * quarter))
    col_norm = jnp.sqrt(col_sq + 1e-06)
    scale_table = magnitude / col_norm
    upper, rest = split_parts(scale_table)
    middle, last = split_parts(scale_table - wide(upper))
    table = jnp.concatenate([upper, middle, last], axis=0)
    hot3 = jnp.concatenate([own.astype(BF)] * 3, axis=1)

    tok_blocks = tokens.reshape(SIDE, block, depth)
    low_blocks = low.reshape(SIDE, block, flat)
    grad_blocks = grad_out.reshape(SIDE, block, cols)
    hot_rows = jnp.pad(own.astype(BF), ((0, 0), (0, 16 - adapters))).T
    hot_blocks = hot_rows.reshape(16, SIDE, block).transpose(1, 0, 2)

    def part(stream, blocks):
        return mixed_part(
            stream,
            jnp.stack(blocks).astype(jnp.int32),
            tok_blocks,
            low_blocks,
            hot_blocks,
            grad_blocks,
            frozen,
            adapter_up,
            adapters,
        )

    away, kept = [], []
    for stream, (one, two, _, _) in enumerate(STREAMS):
        me = place[one[0]]
        there = me ^ one[1]
        away.append(part(stream, (there, there ^ two[1])))
    arrived = [swap(sent, order[0]) for (sent, _), order in zip(away, STREAMS, strict=True)]
    for stream, (one, two, _, _) in enumerate(STREAMS):
        me = place[one[0]]
        kept.append(part(stream, (me, me ^ two[1])))
    mag = jnp.concatenate([a[1] + k[1] for a, k in zip(away, kept, strict=True)], axis=1)
    for pairing in (("dp", 1), ("dp", 3), ("y", 1), ("z", 1), ("y", 3), ("z", 3)):
        mag = mag + swap(mag, pairing)

    adapted = jnp.zeros((tok_rows, cols), BF)
    for stream, (one, two, three, four) in enumerate(STREAMS):
        first = stream * width
        me = place[one[0]]
        got = wide(kept[stream][0]) + wide(arrived[stream])
        total = got[:block] + wide(swap(got[block:].astype(BF), two))
        for pairing in (three, four):
            sent = total.astype(BF)
            total = wide(sent) + wide(swap(sent, pairing))
        rows = lax.dynamic_slice_in_dim(hot3, me * block, block, 0)
        done = (dot(rows, table[:, first : first + width]) * total).astype(BF)
        near = swap(done, one)
        far = swap(jnp.concatenate([done, near], axis=0), two)
        there = me ^ two[1]
        for spot, values in (
            (me, done),
            (me ^ one[1], near),
            (there, far[:block]),
            (there ^ one[1], far[block:]),
        ):
            adapted = lax.dynamic_update_slice(adapted, values, (spot * block, first))

    scaled_grad = (wide(grad_out) * dot(hot3, table)).astype(BF)
    down_upper, down_lower = split_parts(down_sum)
    grad_up = dot(down_upper, scaled_grad, FIRST) + dot(down_lower, scaled_grad, FIRST)
    back = jnp.where(slots, dot(scaled_grad, adapter_up, LAST), 0.0)
    back_upper, back_lower = split_parts(back)
    back_down = dot(back_upper, tokens, FIRST) + dot(back_lower, tokens, FIRST)
    input_part = dot(scaled_grad, frozen, LAST) + (
        dot(back_upper, adapter_down, LAST) + dot(back_lower, adapter_down, LAST)
    )
    sent = jnp.concatenate([input_part, back_down], axis=0).astype(BF)
    total = wide(sent) + wide(lax.ppermute(sent, "col", [(0, 1), (1, 0)]))
    input_grad = total[:tok_rows].astype(BF)
    cut = (cols + depth) // 2 // 256 * 256
    one = grad_up[:, :cut]
    two = jnp.concatenate([grad_up[:, cut:], total[tok_rows:]], axis=1)
    for flip in (1, 3):
        sent = one.astype(BF)
        one = wide(sent) + wide(swap(sent, ("dp", flip)))
        sent = two.astype(BF)
        two = wide(sent) + wide(swap(sent, ("dp", 4 - flip)))
    grad_up = jnp.concatenate([one, two[:, : cols - cut]], axis=1)
    grad_down = two[:, cols - cut :].T
    return (adapted, input_grad, grad_down, grad_up, mag / col_norm)


def solution(mesh):
    assert mesh.axis_names == ("dp", "row", "col")
    grid = Mesh(mesh.devices.reshape(SIDE, SIDE, SIDE, 2), ("dp", "z", "y", "col"))
    row = ("z", "y")
    placed = (
        P("dp", row),
        P(row, "col"),
        P(row, None),
        P(None, "col"),
        P(None, "col"),
        P("dp", "col"),
        P(),
        P(),
    )
    return jax.shard_map(
        on_device,
        mesh=grid,
        in_specs=placed,
        out_specs=(P("dp", "col"), P("dp", row), P(row, None), P(None, "col"), P(None, "col")),
        check_vma=False,
    )
```

```python
import functools

import jax
import jax.numpy as jnp
from jax import lax
from jax.experimental import pallas as pl
from jax.experimental.pallas import tpu as pltpu
from jax.sharding import Mesh
from jax.sharding import PartitionSpec as P

BF = jnp.bfloat16
F32 = jnp.float32
SIDE = 4
PLAIN = (((1,), (0,)), ((), ()))
FIRST = (((0,), (0,)), ((), ()))
LAST = (((1,), (1,)), ((), ()))

STREAMS = (
    (("y", 1), ("y", 3), ("z", 1), ("z", 3)),
    (("y", 3), ("y", 1), ("z", 3), ("z", 1)),
    (("z", 1), ("z", 3), ("y", 1), ("y", 3)),
    (("z", 3), ("z", 1), ("y", 3), ("y", 1)),
)
SPAN = 1536


def swap(values, pairing):
    axis, flip = pairing
    return lax.ppermute(values, axis, [(i, i ^ flip) for i in range(SIDE)])


def wide(values):
    return values.astype(F32)


def dot(a, b, dims=PLAIN):
    return lax.dot_general(a, b, dims, preferred_element_type=F32)


def split_parts(values):
    upper = values.astype(BF)
    return upper, (values - wide(upper)).astype(BF)


def round_bf(values):
    return lax.reduce_precision(values, exponent_bits=8, mantissa_bits=7).astype(BF)


def limits(flops, bytes_accessed):
    return dict(
        compiler_params=pltpu.CompilerParams(vmem_limit_bytes=56 << 20),
        cost_estimate=pl.CostEstimate(
            flops=flops, bytes_accessed=bytes_accessed, transcendentals=0
        ),
    )


def forward_kernel(at, lengths, owners, tokens, maps, frozen, up, grad, *rest):
    n = len(STREAMS)
    outs = [rest[3 * s : 3 * s + 3] for s in range(n)]
    hot3, slots, low, hot, total = rest[3 * n :]
    j = pl.program_id(0)
    rows = tokens.shape[0]
    block = rows // SIDE

    @pl.when(j == 0)
    def _():
        flat = slots.shape[1]
        first = at[0] * rows
        down = first + lax.broadcasted_iota(jnp.int32, slots.shape, 0)
        along = first + lax.broadcasted_iota(jnp.int32, hot.shape, 1)
        by_row, by_col = jnp.zeros_like(down), jnp.zeros_like(along)
        begin = jnp.int32(0)
        for tenant in range(lengths.shape[0]):
            by_row = jnp.where(down >= begin, owners[tenant], by_row)
            by_col = jnp.where(along >= begin, owners[tenant], by_col)
            begin = begin + lengths[tenant]
        column = lax.broadcasted_iota(jnp.int32, slots.shape, 1)
        held = jnp.where(by_row == column // (flat // at[1]), 1.0, 0.0)
        slots[...] = held.astype(BF)
        same = by_row[:, : hot3.shape[1]] == column[:, : hot3.shape[1]] % hot.shape[0]
        hot3[...] = jnp.where(same, 1.0, 0.0).astype(BF)
        same = by_col == lax.broadcasted_iota(jnp.int32, hot.shape, 0)
        hot[...] = jnp.where(same, 1.0, 0.0).astype(BF)
        low[...] = (dot(tokens[...], maps[...]) * held).astype(BF)

    total[...] = dot(tokens[...], frozen[...]) + dot(low[...], up[...])
    mag = dot(hot[...], (total[...] * wide(grad[...])).astype(BF)).astype(BF)
    tall = mag.shape[0]

    for s in range(n):

        @pl.when(j == s)
        def _(s=s):
            away, high, near = outs[s]
            away[block : block + tall, :] = mag
            high[:tall, :] = mag
            near[block:, :] = mag
            places = ((away, 0), (away, block + tall), (near, 0), (high, tall))
            for slot, (ref, first) in enumerate(places):
                spot = pl.multiple_of(at[3 + SIDE * s + slot] * block, block)
                ref[first : first + block, :] = total[pl.ds(spot, block), :].astype(BF)


def forward(at, lengths, owners, tokens, maps, frozen, up, grad):
    rows, depth = tokens.shape
    flat, cols = up.shape
    block = rows // SIDE
    width = cols // len(STREAMS)
    tall = 16

    def whole(shape):
        return pl.BlockSpec(shape, lambda j, *_: (0, 0))

    def moving(height):
        return pl.BlockSpec((height, width), lambda j, *_: (0, j))

    heights = (2 * block + tall, block + tall, block + tall) * len(STREAMS)
    shapes = [(height, width) for height in heights] + [(rows, 3 * tall), (rows, flat)]
    found = pl.pallas_call(
        forward_kernel,
        grid_spec=pltpu.PrefetchScalarGridSpec(
            num_scalar_prefetch=3,
            grid=(len(STREAMS),),
            in_specs=[
                whole((rows, depth)),
                whole((depth, flat)),
                moving(depth),
                moving(flat),
                moving(rows),
            ],
            out_specs=[whole(shape) for shape in shapes],
            scratch_shapes=[
                pltpu.VMEM((rows, flat), BF),
                pltpu.VMEM((tall, rows), BF),
                pltpu.VMEM((rows, width), F32),
            ],
        ),
        out_shape=[jax.ShapeDtypeStruct(shape, BF) for shape in shapes],
        name="forward",
        **limits(2 * rows * (depth + 2 * flat) * cols, 2 * cols * (depth + 2 * rows)),
    )(at, lengths, owners, tokens, maps, frozen, up, grad)
    return [found[3 * s : 3 * s + 3] for s in range(len(STREAMS))], found[-2], found[-1]


def squares_kernel(adapters, tokens, maps, slots, frozen, up, small, left, gram):
    j = pl.program_id(0)
    rows = tokens.shape[0]
    flat = up.shape[0]
    rank = flat // adapters
    pieces = frozen.shape[1] // flat
    size = pieces * adapters

    @pl.when(j == 0)
    def _():
        down = maps[...]
        left[...] = wide(down).T.astype(BF)
        small[:rows, :] = (dot(tokens[...], down) * wide(slots[...])).astype(BF)
        products = dot(left[...], down)
        by_row = lax.broadcasted_iota(jnp.int32, (flat, flat), 0) // rank
        by_col = lax.broadcasted_iota(jnp.int32, (flat, flat), 1) // rank
        upper, lower = split_parts(jnp.where(by_row == by_col, products, 0.0))
        gram[:flat, :] = upper
        gram[flat:, :] = lower

    weights, outer = frozen[...], up[...]
    gram_up = dot(gram[...], outer)
    terms = wide(outer) * (2.0 * dot(left[...], weights) + gram_up[:flat] + gram_up[flat:])
    value = jnp.sum(jnp.square(wide(weights)), axis=0, keepdims=True)
    value = value + jnp.sum(terms.reshape(adapters, rank, -1), axis=1)
    value = jnp.concatenate([value[:, i * flat : (i + 1) * flat] for i in range(pieces)], axis=0)
    small[pl.ds(pl.multiple_of(rows + j * size, 16), size), :] = value.astype(BF)


def column_squares(tokens, maps, slots, frozen, up, adapters):
    rows, depth = tokens.shape
    flat, cols = up.shape

    def whole(values):
        return pl.BlockSpec(values.shape, lambda j: (0, 0))

    def moving(height):
        return pl.BlockSpec((height, SPAN), lambda j: (0, j))

    shape = (rows + cols * adapters // flat, flat)
    return pl.pallas_call(
        functools.partial(squares_kernel, adapters),
        grid=(cols // SPAN,),
        in_specs=[whole(tokens), whole(maps), whole(slots), moving(depth), moving(flat)],
        out_specs=pl.BlockSpec(shape, lambda j: (0, 0)),
        out_shape=jax.ShapeDtypeStruct(shape, BF),
        scratch_shapes=[pltpu.VMEM((flat, depth), BF), pltpu.VMEM((2 * flat, flat), BF)],
        name="squares",
        **limits(2 * flat * depth * cols, 2 * cols * depth),
    )(tokens, maps, slots, frozen, up)


def place(at, parts, height, out_shape, onto=None, after=()):
    flat = [values for part in parts for values in part]
    count = len(flat) // len(STREAMS)

    def kernel(at, *refs):
        out, sems = refs[-2:]
        width = out.shape[1] // len(STREAMS)
        copies = []
        for s in range(len(STREAMS)):
            for values in refs[s * count : (s + 1) * count]:
                for first in range(0, values.shape[0], height):
                    spot = pl.multiple_of(at[len(copies)] * height, height)
                    copies.append(
                        pltpu.make_async_copy(
                            values.at[pl.ds(first, height), :],
                            out.at[pl.ds(spot, height), pl.ds(s * width, width)],
                            sems.at[len(copies)],
                        )
                    )
        for copy in copies:
            copy.start()
        for copy in copies:
            copy.wait()

    anywhere = pl.BlockSpec(memory_space=pl.ANY)
    more = list(after) + ([onto] if onto is not None else [])
    return pl.pallas_call(
        kernel,
        in_specs=[pl.BlockSpec(memory_space=pltpu.SMEM)]
        + [pl.BlockSpec(memory_space=pltpu.VMEM)] * len(flat)
        + [anywhere] * len(more),
        out_specs=anywhere,
        out_shape=out_shape,
        scratch_shapes=[pltpu.SemaphoreType.DMA((2 * len(STREAMS),))],
        input_output_aliases={1 + len(flat) + len(after): 0} if onto is not None else {},
        compiler_params=pltpu.CompilerParams(vmem_limit_bytes=12 << 20),
        name="place",
    )(at, *flat, *more)


def table_kernel(rows, mine, got, magnitude, table, norm, down):
    adapters, cols = magnitude.shape
    flat = mine.shape[1]
    total = wide(mine[...]) + wide(got[...])
    down[...] = total[:rows].astype(BF)
    for i in range(cols // flat):
        first = i * flat
        here = jnp.sqrt(total[rows + i * adapters : rows + (i + 1) * adapters] + 1e-06)
        norm[:, first : first + flat] = here
        scale = magnitude[:, first : first + flat] / here
        for part in range(3):
            taken = wide(scale.astype(BF))
            scale = scale - taken
            padded = jnp.concatenate([taken, jnp.zeros_like(taken)], axis=0)
            table[16 * part : 16 * part + 16, first : first + flat] = padded.astype(BF)


def grad_up_kernel(at, grad, table, hot, down, out):
    scaled = (wide(grad[...]) * dot(hot[...], table[...])).astype(BF)
    out[...] = dot(down[...], scaled, FIRST)


def grad_up_part(at, grad, table, hot, down, share):
    flat = down.shape[1]

    def mine(values):
        return pl.BlockSpec((values.shape[0], share), lambda j, at: (0, at[2]))

    def whole(values):
        return pl.BlockSpec(values.shape, lambda j, at: (0, 0))

    return pl.pallas_call(
        grad_up_kernel,
        grid_spec=pltpu.PrefetchScalarGridSpec(
            num_scalar_prefetch=1,
            grid=(1,),
            in_specs=[mine(grad), mine(table), whole(hot), whole(down)],
            out_specs=pl.BlockSpec((flat, share), lambda j, at: (0, 0)),
        ),
        out_shape=jax.ShapeDtypeStruct((flat, share), F32),
        name="grad_up",
        **limits(0, 3 * grad.shape[0] * share),
    )(at, grad, table, hot, down)


def backward_kernel(grad, table, hot, frozen, up, slots, tokens, maps, sent, back, total):
    j = pl.program_id(0)
    rows = hot.shape[0]

    @pl.when(j == 0)
    def _():
        back[...] = jnp.zeros_like(back)
        total[...] = jnp.zeros_like(total)

    scaled = (wide(grad[...]) * dot(hot[...], table[...])).astype(BF)
    back[...] += dot(scaled, up[...], LAST)
    total[...] += dot(scaled, frozen[...], LAST)

    @pl.when(j == pl.num_programs(0) - 1)
    def _():
        upper, lower = split_parts(back[...] * wide(slots[...]))
        down_maps = maps[...]
        full = total[...] + dot(upper, down_maps, LAST) + dot(lower, down_maps, LAST)
        sent[:rows, :] = full.astype(BF)
        values = tokens[...]
        sent[rows:, :] = (dot(upper, values, FIRST) + dot(lower, values, FIRST)).astype(BF)


def backward(grad, table, hot, frozen, up, slots, tokens, maps):
    rows, depth = tokens.shape
    flat, cols = up.shape

    def whole(values):
        return pl.BlockSpec(values.shape, lambda j: (0, 0))

    def moving(height):
        return pl.BlockSpec((height, SPAN), lambda j: (0, j))

    return pl.pallas_call(
        backward_kernel,
        grid=(cols // SPAN,),
        in_specs=[
            moving(rows),
            moving(table.shape[0]),
            whole(hot),
            moving(depth),
            moving(flat),
            whole(slots),
            whole(tokens),
            whole(maps),
        ],
        out_specs=pl.BlockSpec((rows + flat, depth), lambda j: (0, 0)),
        out_shape=jax.ShapeDtypeStruct((rows + flat, depth), BF),
        scratch_shapes=[pltpu.VMEM((rows, flat), F32), pltpu.VMEM((rows, depth), F32)],
        name="backward",
        **limits(2 * rows * (depth + 2 * flat) * cols, 2 * cols * (depth + rows)),
    )(grad, table, hot, frozen, up, slots, tokens, maps)


def on_device(
    tokens, frozen, adapter_down, adapter_up, magnitude, grad_out, tenant_lengths, tenant_adapter
):
    tok_rows, depth = tokens.shape
    adapters, cols = magnitude.shape
    flat = adapter_down.shape[1]
    block = tok_rows // SIDE
    width = cols // len(STREAMS)
    spot = {axis: lax.axis_index(axis) for axis in ("dp", "z", "y")}

    spots = [spot["dp"], jnp.int32(adapters), spot["z"] * SIDE + spot["y"]]
    early, late = [], []
    for one, two, _, _ in STREAMS:
        me = spot[one[0]]
        there = me ^ one[1]
        spots += [there, there ^ two[1], me, me ^ two[1]]
        early += [me, there]
        late += [me ^ two[1], there ^ two[1]]
    at, early, late = (jnp.stack(v).astype(jnp.int32) for v in (spots, early, late))
    streams, hot3, slots = forward(
        at, tenant_lengths, tenant_adapter, tokens, adapter_down, frozen, adapter_up, grad_out
    )
    small = column_squares(tokens, adapter_down, slots, frozen, adapter_up, adapters)

    def exchange(values, step):
        return [swap(v, order[step]) for v, order in zip(values, STREAMS, strict=True)]

    first = exchange([away for away, _, _ in streams], 0)
    for step, pairing in enumerate((("y", 1), ("z", 1), ("y", 3), ("z", 3))):
        if step == 0:
            small, _ = lax.optimization_barrier((small, first))
        got = swap(small, pairing)
        if step < 3:
            small = round_bf(wide(small) + wide(got))
    table, col_norm, down = pl.pallas_call(
        functools.partial(table_kernel, tok_rows),
        out_shape=[
            jax.ShapeDtypeStruct((48, cols), BF),
            jax.ShapeDtypeStruct((adapters, cols), F32),
            jax.ShapeDtypeStruct((tok_rows, flat), BF),
        ],
        name="table",
        compiler_params=pltpu.CompilerParams(vmem_limit_bytes=12 << 20),
    )(small, got, magnitude)

    tall = hot3.shape[1] // 3
    sums = [
        round_bf(wide(high) + wide(got[block:]))
        for (_, high, _), got in zip(streams, first, strict=True)
    ]
    second = exchange(sums, 1)
    sums = [
        round_bf(
            jnp.concatenate(
                [
                    wide(near[:block]) + wide(got[:block]) + wide(more[tall:]),
                    wide(summed[:tall]) + wide(more[:tall]),
                ],
                axis=0,
            )
        )
        for (_, _, near), got, summed, more in zip(streams, first, sums, second, strict=True)
    ]
    got = exchange(sums, 2)
    sums = [round_bf(wide(a) + wide(b)) for a, b in zip(sums, got, strict=True)]
    got = exchange(sums, 3)
    done, mags = [], []
    for s, (a, b) in enumerate(zip(sums, got, strict=True)):
        me = spot[STREAMS[s][0][0]]
        rows = lax.dynamic_slice_in_dim(hot3, me * block, block, 0)
        scale = dot(rows, table[:, s * width : (s + 1) * width])
        done.append((scale * (wide(a[:block]) + wide(b[:block]))).astype(BF))
        mags.append(wide(a[block : block + adapters]) + wide(b[block : block + adapters]))
    near = exchange(done, 0)
    sent = backward(grad_out, table, hot3, frozen, adapter_up, slots, tokens, adapter_down)
    near, sent = lax.optimization_barrier((near, sent))
    pairs = [jnp.concatenate(both, axis=0) for both in zip(done, near, strict=True)]
    far = exchange(pairs, 1)
    mag = jnp.concatenate(mags, axis=1)
    for flip in (1, 3):
        mag = mag + swap(mag, ("dp", flip))

    grad_up = grad_up_part(at, grad_out, table, hot3, down, cols // SIDE**2)
    for flip in (1, 3):
        grad_up = grad_up + swap(grad_up, ("dp", flip))
    grad_up = lax.all_gather(round_bf(grad_up), ("z", "y"), axis=1, tiled=True).astype(F32)
    total = wide(sent) + wide(lax.ppermute(sent, "col", [(0, 1), (1, 0)]))
    input_grad = total[:tok_rows].astype(BF)
    grad_down = total[tok_rows:]
    for flip in (1, 3):
        share = round_bf(grad_down)
        grad_down = wide(share) + wide(swap(share, ("dp", flip)))
    whole = jax.ShapeDtypeStruct((tok_rows, cols), BF)
    adapted = place(early, list(zip(done, near, strict=True)), block, whole)
    adapted = place(late, [[v] for v in far], block, whole, onto=adapted, after=(grad_up,))
    return (adapted, input_grad, grad_down.T, grad_up, mag / col_norm)


def solution(mesh):
    assert mesh.axis_names == ("dp", "row", "col")
    grid = Mesh(mesh.devices.reshape(SIDE, SIDE, SIDE, 2), ("dp", "z", "y", "col"))
    row = ("z", "y")
    placed = (
        P("dp", row),
        P(row, "col"),
        P(row, None),
        P(None, "col"),
        P(None, "col"),
        P("dp", "col"),
        P(),
        P(),
    )
    return jax.shard_map(
        on_device,
        mesh=grid,
        in_specs=placed,
        out_specs=(P("dp", "col"), P("dp", row), P(row, None), P(None, "col"), P(None, "col")),
        check_vma=False,
    )
```

```python
import functools

import jax
import jax.numpy as jnp
from jax import lax
from jax.experimental import pallas as pl
from jax.experimental.pallas import tpu as pltpu
from jax.sharding import Mesh
from jax.sharding import PartitionSpec as P

BF = jnp.bfloat16
F32 = jnp.float32
SIDE = 4
PLAIN = (((1,), (0,)), ((), ()))
FIRST = (((0,), (0,)), ((), ()))
LAST = (((1,), (1,)), ((), ()))

STREAMS = (
    (("y", 1), ("y", 3), ("z", 1), ("z", 3)),
    (("y", 3), ("y", 1), ("z", 3), ("z", 1)),
    (("z", 1), ("z", 3), ("y", 1), ("y", 3)),
    (("z", 3), ("z", 1), ("y", 3), ("y", 1)),
)
SPAN = 1536


def swap(values, pairing):
    axis, flip = pairing
    return lax.ppermute(values, axis, [(i, i ^ flip) for i in range(SIDE)])


def wide(values):
    return values.astype(F32)


def dot(a, b, dims=PLAIN):
    return lax.dot_general(a, b, dims, preferred_element_type=F32)


def split_parts(values):
    upper = values.astype(BF)
    return upper, (values - wide(upper)).astype(BF)


def round_bf(values):
    return lax.reduce_precision(values, exponent_bits=8, mantissa_bits=7).astype(BF)


def limits(flops, bytes_accessed):
    return dict(
        compiler_params=pltpu.CompilerParams(vmem_limit_bytes=56 << 20),
        cost_estimate=pl.CostEstimate(
            flops=flops, bytes_accessed=bytes_accessed, transcendentals=0
        ),
    )


def forward_kernel(at, lengths, owners, tokens, maps, frozen, up, grad, *rest):
    n = len(STREAMS)
    outs = [rest[3 * s : 3 * s + 3] for s in range(n)]
    hot3, slots, low, hot, total = rest[3 * n :]
    j = pl.program_id(0)
    rows = tokens.shape[0]
    block = rows // SIDE

    @pl.when(j == 0)
    def _():
        flat = slots.shape[1]
        first = at[0] * rows
        down = first + lax.broadcasted_iota(jnp.int32, slots.shape, 0)
        along = first + lax.broadcasted_iota(jnp.int32, hot.shape, 1)
        by_row, by_col = jnp.zeros_like(down), jnp.zeros_like(along)
        begin = jnp.int32(0)
        for tenant in range(lengths.shape[0]):
            by_row = jnp.where(down >= begin, owners[tenant], by_row)
            by_col = jnp.where(along >= begin, owners[tenant], by_col)
            begin = begin + lengths[tenant]
        column = lax.broadcasted_iota(jnp.int32, slots.shape, 1)
        held = jnp.where(by_row == column // (flat // at[1]), 1.0, 0.0)
        slots[...] = held.astype(BF)
        same = by_row[:, : hot3.shape[1]] == column[:, : hot3.shape[1]] % hot.shape[0]
        hot3[...] = jnp.where(same, 1.0, 0.0).astype(BF)
        same = by_col == lax.broadcasted_iota(jnp.int32, hot.shape, 0)
        hot[...] = jnp.where(same, 1.0, 0.0).astype(BF)
        low[...] = (dot(tokens[...], maps[...]) * held).astype(BF)

    total[...] = dot(tokens[...], frozen[...]) + dot(low[...], up[...])
    mag = dot(hot[...], (total[...] * wide(grad[...])).astype(BF)).astype(BF)
    tall = mag.shape[0]

    for s in range(n):

        @pl.when(j == s)
        def _(s=s):
            away, high, near = outs[s]
            away[block : block + tall, :] = mag
            high[:tall, :] = mag
            near[block:, :] = mag
            places = ((away, 0), (away, block + tall), (near, 0), (high, tall))
            for slot, (ref, first) in enumerate(places):
                spot = pl.multiple_of(at[3 + SIDE * s + slot] * block, block)
                ref[first : first + block, :] = total[pl.ds(spot, block), :].astype(BF)


def forward(at, lengths, owners, tokens, maps, frozen, up, grad):
    rows, depth = tokens.shape
    flat, cols = up.shape
    block = rows // SIDE
    width = cols // len(STREAMS)
    tall = 16

    def whole(shape):
        return pl.BlockSpec(shape, lambda j, *_: (0, 0))

    def moving(height):
        return pl.BlockSpec((height, width), lambda j, *_: (0, j))

    heights = (2 * block + tall, block + tall, block + tall) * len(STREAMS)
    shapes = [(height, width) for height in heights] + [(rows, 3 * tall), (rows, flat)]
    found = pl.pallas_call(
        forward_kernel,
        grid_spec=pltpu.PrefetchScalarGridSpec(
            num_scalar_prefetch=3,
            grid=(len(STREAMS),),
            in_specs=[
                whole((rows, depth)),
                whole((depth, flat)),
                moving(depth),
                moving(flat),
                moving(rows),
            ],
            out_specs=[whole(shape) for shape in shapes],
            scratch_shapes=[
                pltpu.VMEM((rows, flat), BF),
                pltpu.VMEM((tall, rows), BF),
                pltpu.VMEM((rows, width), F32),
            ],
        ),
        out_shape=[jax.ShapeDtypeStruct(shape, BF) for shape in shapes],
        name="forward",
        **limits(2 * rows * (depth + 2 * flat) * cols, 2 * cols * (depth + 2 * rows)),
    )(at, lengths, owners, tokens, maps, frozen, up, grad)
    return [found[3 * s : 3 * s + 3] for s in range(len(STREAMS))], found[-2], found[-1]


def squares_kernel(adapters, tokens, maps, slots, frozen, up, small, left, gram):
    j = pl.program_id(0)
    rows = tokens.shape[0]
    flat = up.shape[0]
    rank = flat // adapters
    pieces = frozen.shape[1] // flat
    size = pieces * adapters

    @pl.when(j == 0)
    def _():
        down = maps[...]
        left[...] = wide(down).T.astype(BF)
        small[:rows, :] = (dot(tokens[...], down) * wide(slots[...])).astype(BF)
        products = dot(left[...], down)
        by_row = lax.broadcasted_iota(jnp.int32, (flat, flat), 0) // rank
        by_col = lax.broadcasted_iota(jnp.int32, (flat, flat), 1) // rank
        upper, lower = split_parts(jnp.where(by_row == by_col, products, 0.0))
        gram[:flat, :] = upper
        gram[flat:, :] = lower

    weights, outer = frozen[...], up[...]
    gram_up = dot(gram[...], outer)
    terms = wide(outer) * (2.0 * dot(left[...], weights) + gram_up[:flat] + gram_up[flat:])
    value = jnp.sum(jnp.square(wide(weights)), axis=0, keepdims=True)
    value = value + jnp.sum(terms.reshape(adapters, rank, -1), axis=1)
    value = jnp.concatenate([value[:, i * flat : (i + 1) * flat] for i in range(pieces)], axis=0)
    small[pl.ds(pl.multiple_of(rows + j * size, 16), size), :] = value.astype(BF)


def column_squares(tokens, maps, slots, frozen, up, adapters):
    rows, depth = tokens.shape
    flat, cols = up.shape

    def whole(values):
        return pl.BlockSpec(values.shape, lambda j: (0, 0))

    def moving(height):
        return pl.BlockSpec((height, SPAN), lambda j: (0, j))

    shape = (rows + cols * adapters // flat, flat)
    return pl.pallas_call(
        functools.partial(squares_kernel, adapters),
        grid=(cols // SPAN,),
        in_specs=[whole(tokens), whole(maps), whole(slots), moving(depth), moving(flat)],
        out_specs=pl.BlockSpec(shape, lambda j: (0, 0)),
        out_shape=jax.ShapeDtypeStruct(shape, BF),
        scratch_shapes=[pltpu.VMEM((flat, depth), BF), pltpu.VMEM((2 * flat, flat), BF)],
        name="squares",
        **limits(2 * flat * depth * cols, 2 * cols * depth),
    )(tokens, maps, slots, frozen, up)


def place(at, parts, height, out_shape, onto=None, after=(), begin=0):
    flat = [values for part in parts for values in part]
    count = len(flat) // len(parts)

    def kernel(at, *refs):
        out, sems = refs[-2:]
        width = out.shape[1] // len(STREAMS)
        copies = []
        for s in range(len(parts)):
            for values in refs[s * count : (s + 1) * count]:
                for first in range(0, values.shape[0], height):
                    spot = pl.multiple_of(at[len(copies)] * height, height)
                    copies.append(
                        pltpu.make_async_copy(
                            values.at[pl.ds(first, height), :],
                            out.at[pl.ds(spot, height), pl.ds((begin + s) * width, width)],
                            sems.at[len(copies)],
                        )
                    )
        for copy in copies:
            copy.start()
        for copy in copies:
            copy.wait()

    anywhere = pl.BlockSpec(memory_space=pl.ANY)
    more = list(after) + ([onto] if onto is not None else [])
    return pl.pallas_call(
        kernel,
        in_specs=[pl.BlockSpec(memory_space=pltpu.SMEM)]
        + [pl.BlockSpec(memory_space=pltpu.VMEM)] * len(flat)
        + [anywhere] * len(more),
        out_specs=anywhere,
        out_shape=out_shape,
        scratch_shapes=[pltpu.SemaphoreType.DMA((2 * len(parts),))],
        input_output_aliases={1 + len(flat) + len(after): 0} if onto is not None else {},
        compiler_params=pltpu.CompilerParams(vmem_limit_bytes=12 << 20),
        name="place",
    )(at, *flat, *more)


def table_kernel(rows, mine, got, magnitude, table, norm, down):
    adapters, cols = magnitude.shape
    flat = mine.shape[1]
    total = wide(mine[...]) + wide(got[...])
    down[...] = total[:rows].astype(BF)
    for i in range(cols // flat):
        first = i * flat
        here = jnp.sqrt(total[rows + i * adapters : rows + (i + 1) * adapters] + 1e-06)
        norm[:, first : first + flat] = here
        scale = magnitude[:, first : first + flat] / here
        for part in range(3):
            taken = wide(scale.astype(BF))
            scale = scale - taken
            padded = jnp.concatenate([taken, jnp.zeros_like(taken)], axis=0)
            table[16 * part : 16 * part + 16, first : first + flat] = padded.astype(BF)


def grad_up_kernel(at, grad, table, hot, down, out):
    scaled = (wide(grad[...]) * dot(hot[...], table[...])).astype(BF)
    out[...] = dot(down[...], scaled, FIRST)


def grad_up_part(at, grad, table, hot, down, share):
    flat = down.shape[1]

    def mine(values):
        return pl.BlockSpec((values.shape[0], share), lambda j, at: (0, at[2]))

    def whole(values):
        return pl.BlockSpec(values.shape, lambda j, at: (0, 0))

    return pl.pallas_call(
        grad_up_kernel,
        grid_spec=pltpu.PrefetchScalarGridSpec(
            num_scalar_prefetch=1,
            grid=(1,),
            in_specs=[mine(grad), mine(table), whole(hot), whole(down)],
            out_specs=pl.BlockSpec((flat, share), lambda j, at: (0, 0)),
        ),
        out_shape=jax.ShapeDtypeStruct((flat, share), F32),
        name="grad_up",
        **limits(0, 3 * grad.shape[0] * share),
    )(at, grad, table, hot, down)


def back_kernel(grad, table, hot, up, slots, tokens, maps, *rest):
    parts, (packed, low, scaled, back) = rest[:-4], rest[-4:]
    j = pl.program_id(0)
    adapters = parts[0].shape[0] // 2
    depth = tokens.shape[1]

    @pl.when(j == 0)
    def _():
        back[...] = jnp.zeros_like(back)

    scaled[...] = (wide(grad[...]) * dot(hot[...], table[...])).astype(BF)
    back[...] += dot(scaled[...], up[...], LAST)

    @pl.when(j == pl.num_programs(0) - 1)
    def _():
        upper, lower = split_parts(back[...] * wide(slots[...]))
        low[...] = dot(upper, maps[...], LAST) + dot(lower, maps[...], LAST)
        values = tokens[...]
        packed[:, :depth] = (dot(upper, values, FIRST) + dot(lower, values, FIRST)).astype(BF)
        size = packed.shape[1] - depth
        for s in range(len(STREAMS)):
            total = wide(parts[2 * s][...]) + wide(parts[2 * s + 1][...])
            for q in range(total.shape[1] // size // 2):
                first = 2 * q * size
                both = [total[:adapters, first + k * size : first + (k + 1) * size] for k in (0, 1)]
                at = (s * (total.shape[1] // size) + 2 * q) * adapters
                packed[at : at + 2 * adapters, depth:] = jnp.concatenate(both, axis=0).astype(BF)


def back_part(grad, table, hot, up, slots, tokens, maps, parts, share):
    rows, cols = grad.shape
    depth, flat = maps.shape
    tall = hot.shape[1] // 3

    def whole(shape):
        return pl.BlockSpec(shape, lambda j: (0, 0))

    def moving(values):
        return pl.BlockSpec((values.shape[0], SPAN), lambda j: (0, j))

    def foot(values):
        return pl.BlockSpec((tall, values.shape[1]), lambda j: (values.shape[0] // tall - 1, 0))

    return pl.pallas_call(
        back_kernel,
        grid=(cols // SPAN,),
        in_specs=[moving(grad), moving(table), whole(hot.shape), moving(up)]
        + [whole(values.shape) for values in (slots, tokens, maps)]
        + [foot(values) for values in parts],
        out_specs=[whole((flat, depth + share)), whole((rows, depth)), moving(grad)],
        out_shape=[
            jax.ShapeDtypeStruct((flat, depth + share), BF),
            jax.ShapeDtypeStruct((rows, depth), F32),
            jax.ShapeDtypeStruct((rows, cols), BF),
        ],
        scratch_shapes=[pltpu.VMEM((rows, flat), F32)],
        name="back",
        **limits(2 * rows * 2 * flat * cols, 2 * cols * rows),
    )(grad, table, hot, up, slots, tokens, maps, *parts)


def backward_kernel(scaled, frozen, start, out, total):
    j = pl.program_id(0)

    @pl.when(j == 0)
    def _():
        total[...] = start[...]

    total[...] += dot(scaled[...], frozen[...], LAST)

    @pl.when(j == pl.num_programs(0) - 1)
    def _():
        out[...] = total[...].astype(BF)


def backward(scaled, frozen, start):
    rows, cols = scaled.shape
    depth = frozen.shape[0]
    span = cols // 3

    def whole(shape):
        return pl.BlockSpec(shape, lambda j: (0, 0))

    def moving(values):
        return pl.BlockSpec((values.shape[0], span), lambda j: (0, j))

    return pl.pallas_call(
        backward_kernel,
        grid=(3,),
        in_specs=[moving(scaled), moving(frozen), whole(start.shape)],
        out_specs=whole(start.shape),
        out_shape=jax.ShapeDtypeStruct(start.shape, BF),
        scratch_shapes=[pltpu.VMEM((rows, depth), F32)],
        name="backward",
        **limits(2 * rows * depth * cols, 2 * cols * (depth + rows)),
    )(scaled, frozen, start)


def on_device(
    tokens, frozen, adapter_down, adapter_up, magnitude, grad_out, tenant_lengths, tenant_adapter
):
    tok_rows, depth = tokens.shape
    adapters, cols = magnitude.shape
    flat = adapter_down.shape[1]
    block = tok_rows // SIDE
    width = cols // len(STREAMS)
    spot = {axis: lax.axis_index(axis) for axis in ("dp", "z", "y")}

    spots = [spot["dp"], jnp.int32(adapters), spot["z"] * SIDE + spot["y"]]
    early, late = [], []
    for one, two, _, _ in STREAMS:
        me = spot[one[0]]
        there = me ^ one[1]
        spots += [there, there ^ two[1], me, me ^ two[1]]
        early += [me, there]
        late += [me ^ two[1], there ^ two[1]]
    at, early, late = (jnp.stack(v).astype(jnp.int32) for v in (spots, early, late))
    streams, hot3, slots = forward(
        at, tenant_lengths, tenant_adapter, tokens, adapter_down, frozen, adapter_up, grad_out
    )
    small = column_squares(tokens, adapter_down, slots, frozen, adapter_up, adapters)

    def exchange(values, step):
        return [swap(v, order[step]) for v, order in zip(values, STREAMS, strict=True)]

    first = exchange([away for away, _, _ in streams], 0)
    for step, pairing in enumerate((("y", 1), ("z", 1), ("y", 3), ("z", 3))):
        if step == 0:
            small, _ = lax.optimization_barrier((small, first[0]))
        got = swap(small, pairing)
        if step < 3:
            small = round_bf(wide(small) + wide(got))
    table, col_norm, down = pl.pallas_call(
        functools.partial(table_kernel, tok_rows),
        out_shape=[
            jax.ShapeDtypeStruct((48, cols), BF),
            jax.ShapeDtypeStruct((adapters, cols), F32),
            jax.ShapeDtypeStruct((tok_rows, flat), BF),
        ],
        name="table",
        compiler_params=pltpu.CompilerParams(vmem_limit_bytes=12 << 20),
    )(small, got, magnitude)

    tall = hot3.shape[1] // 3
    sums = [
        round_bf(wide(high) + wide(got[block:]))
        for (_, high, _), got in zip(streams, first, strict=True)
    ]
    second = exchange(sums, 1)
    sums = [
        round_bf(
            jnp.concatenate(
                [
                    wide(near[:block]) + wide(got[:block]) + wide(more[tall:]),
                    wide(summed[:tall]) + wide(more[:tall]),
                ],
                axis=0,
            )
        )
        for (_, _, near), got, summed, more in zip(streams, first, sums, second, strict=True)
    ]
    got = exchange(sums, 2)
    sums = [round_bf(wide(a) + wide(b)) for a, b in zip(sums, got, strict=True)]
    got = exchange(sums, 3)

    grad_up = grad_up_part(at, grad_out, table, hot3, down, cols // SIDE**2)
    for flip in (1, 3):
        grad_up = grad_up + swap(grad_up, ("dp", flip))
    share = round_bf(grad_up)

    done = []
    for s, (a, b) in enumerate(zip(sums, got, strict=True)):
        me = spot[STREAMS[s][0][0]]
        rows = lax.dynamic_slice_in_dim(hot3, me * block, block, 0)
        scale = dot(rows, table[:, s * width : (s + 1) * width])
        done.append((scale * (wide(a[:block]) + wide(b[:block]))).astype(BF))
    near = exchange(done, 0)
    parts = [v for both in zip(sums, got, strict=True) for v in both]
    packed, low, scaled = back_part(
        grad_out, table, hot3, adapter_up, slots, tokens, adapter_down, parts, cols // SIDE**2
    )
    near, packed, low = lax.optimization_barrier((near, packed, low))
    packed = round_bf(wide(packed) + wide(swap(packed, ("dp", 1))))
    low, packed = lax.optimization_barrier((low, packed))
    pairs = [jnp.concatenate(both, axis=0) for both in zip(done, near, strict=True)]
    far = exchange(pairs, 1)
    grad_up = lax.all_gather(share, ("z", "y"), axis=1, tiled=True).astype(F32)
    packed = wide(packed) + wide(swap(packed, ("dp", 3)))
    mag = packed[:, depth:].reshape(-1, adapters, packed.shape[1] - depth)
    mag = mag.transpose(1, 0, 2).reshape(adapters, cols)
    sent = backward(scaled, frozen, low)
    sent = jnp.concatenate([sent, round_bf(packed[:, :depth])] * 2, axis=0)
    both = wide(lax.all_to_all(sent, "col", 0, 0, tiled=True))
    total = both[: tok_rows + flat] + both[tok_rows + flat :]
    input_grad = total[:tok_rows].astype(BF)
    grad_down = total[tok_rows:]
    whole = jax.ShapeDtypeStruct((tok_rows, cols), BF)
    adapted = place(early, list(zip(done, near, strict=True)), block, whole)
    after = (grad_up, input_grad)
    adapted = place(late, [[v] for v in far], block, whole, onto=adapted, after=after)
    return (adapted, input_grad, grad_down.T, grad_up, mag / col_norm)


def solution(mesh):
    assert mesh.axis_names == ("dp", "row", "col")
    grid = Mesh(mesh.devices.reshape(SIDE, SIDE, SIDE, 2), ("dp", "z", "y", "col"))
    row = ("z", "y")
    placed = (
        P("dp", row),
        P(row, "col"),
        P(row, None),
        P(None, "col"),
        P(None, "col"),
        P("dp", "col"),
        P(),
        P(),
    )
    return jax.shard_map(
        on_device,
        mesh=grid,
        in_specs=placed,
        out_specs=(P("dp", "col"), P("dp", row), P(row, None), P(None, "col"), P(None, "col")),
        check_vma=False,
    )
```

```python
import functools

import jax
import jax.numpy as jnp
from jax import lax
from jax.experimental import pallas as pl
from jax.experimental.pallas import tpu as pltpu
from jax.sharding import Mesh
from jax.sharding import PartitionSpec as P

BF = jnp.bfloat16
F32 = jnp.float32
SIDE = 4
PLAIN = (((1,), (0,)), ((), ()))
FIRST = (((0,), (0,)), ((), ()))
LAST = (((1,), (1,)), ((), ()))

STREAMS = (
    (("y", 1), ("y", 3), ("z", 1), ("z", 3)),
    (("y", 3), ("y", 1), ("z", 3), ("z", 1)),
    (("z", 1), ("z", 3), ("y", 1), ("y", 3)),
    (("z", 3), ("z", 1), ("y", 3), ("y", 1)),
)
SPAN = 1536


def swap(values, pairing):
    axis, flip = pairing
    return lax.ppermute(values, axis, [(i, i ^ flip) for i in range(SIDE)])


def wide(values):
    return values.astype(F32)


def dot(a, b, dims=PLAIN):
    return lax.dot_general(a, b, dims, preferred_element_type=F32)


def split_parts(values):
    upper = values.astype(BF)
    return upper, (values - wide(upper)).astype(BF)


def round_bf(values):
    return lax.reduce_precision(values, exponent_bits=8, mantissa_bits=7).astype(BF)


def limits(flops, bytes_accessed):
    return dict(
        compiler_params=pltpu.CompilerParams(vmem_limit_bytes=56 << 20),
        cost_estimate=pl.CostEstimate(
            flops=flops, bytes_accessed=bytes_accessed, transcendentals=0
        ),
    )


def forward_kernel(at, lengths, owners, tokens, maps, frozen, up, grad, *rest):
    n = len(STREAMS)
    outs = [rest[3 * s : 3 * s + 3] for s in range(n)]
    hot3, slots, low, hot, stage, sems = rest[3 * n :]
    j = pl.program_id(0)
    rows = tokens.shape[0]
    block = rows // SIDE

    @pl.when(j == 0)
    def _():
        flat = slots.shape[1]
        first = at[0] * rows
        down = first + lax.broadcasted_iota(jnp.int32, slots.shape, 0)
        along = first + lax.broadcasted_iota(jnp.int32, hot.shape, 1)
        by_row, by_col = jnp.zeros_like(down), jnp.zeros_like(along)
        begin = jnp.int32(0)
        for tenant in range(lengths.shape[0]):
            by_row = jnp.where(down >= begin, owners[tenant], by_row)
            by_col = jnp.where(along >= begin, owners[tenant], by_col)
            begin = begin + lengths[tenant]
        column = lax.broadcasted_iota(jnp.int32, slots.shape, 1)
        held = jnp.where(by_row == column // (flat // at[1]), 1.0, 0.0)
        slots[...] = held.astype(BF)
        same = by_row[:, : hot3.shape[1]] == column[:, : hot3.shape[1]] % hot.shape[0]
        hot3[...] = jnp.where(same, 1.0, 0.0).astype(BF)
        same = by_col == lax.broadcasted_iota(jnp.int32, hot.shape, 0)
        hot[...] = jnp.where(same, 1.0, 0.0).astype(BF)
        low[...] = (dot(tokens[...], maps[...]) * held).astype(BF)

    total = dot(tokens[...], frozen[...]) + dot(low[...], up[...])
    mag = dot(hot[...], (total * wide(grad[...])).astype(BF)).astype(BF)
    tall = mag.shape[0]

    def copies(s):
        first = 0
        for part, out in enumerate((outs[s][2], outs[s][0], outs[s][1])):
            height = out.shape[0]
            held = stage.at[s % 2, pl.ds(first, height), :]
            yield pltpu.make_async_copy(held, out, sems.at[s % 2, part])
            first += height

    for s in range(n):

        @pl.when(j == s)
        def _(s=s):
            if s >= 2:
                for copy in copies(s - 2):
                    copy.wait()
            for first in (block, 2 * block + tall, 3 * block + 2 * tall):
                stage[s % 2, first : first + tall, :] = mag
            for which in range(SIDE):
                spot = pl.multiple_of(at[3 + SIDE * s + which], 16)
                rows_of = total[which * block : (which + 1) * block]
                stage[s % 2, pl.ds(spot, block), :] = rows_of.astype(BF)
            for copy in copies(s):
                copy.start()
            if s == n - 1:
                for copy in (*copies(s - 1), *copies(s)):
                    copy.wait()


def forward(at, lengths, owners, tokens, maps, frozen, up, grad):
    rows, depth = tokens.shape
    flat, cols = up.shape
    block = rows // SIDE
    width = cols // len(STREAMS)
    tall = 16

    def whole(shape):
        return pl.BlockSpec(shape, lambda j, *_: (0, 0))

    def moving(height):
        return pl.BlockSpec((height, width), lambda j, *_: (0, j))

    heights = (2 * block + tall, block + tall, block + tall) * len(STREAMS)
    shapes = [(height, width) for height in heights] + [(rows, 3 * tall), (rows, flat)]
    found = pl.pallas_call(
        forward_kernel,
        grid_spec=pltpu.PrefetchScalarGridSpec(
            num_scalar_prefetch=3,
            grid=(len(STREAMS),),
            in_specs=[
                whole((rows, depth)),
                whole((depth, flat)),
                moving(depth),
                moving(flat),
                moving(rows),
            ],
            out_specs=[pl.BlockSpec(memory_space=pl.ANY)] * len(heights)
            + [whole(shape) for shape in shapes[len(heights) :]],
            scratch_shapes=[
                pltpu.VMEM((rows, flat), BF),
                pltpu.VMEM((tall, rows), BF),
                pltpu.VMEM((2, rows + 3 * tall, width), BF),
                pltpu.SemaphoreType.DMA((2, 3)),
            ],
        ),
        out_shape=[jax.ShapeDtypeStruct(shape, BF) for shape in shapes],
        name="forward",
        **limits(2 * rows * (depth + 2 * flat) * cols, 2 * cols * (depth + 2 * rows)),
    )(at, lengths, owners, tokens, maps, frozen, up, grad)
    return [found[3 * s : 3 * s + 3] for s in range(len(STREAMS))], found[-2], found[-1]


def squares_kernel(adapters, tokens, maps, slots, frozen, up, small, left, gram):
    j = pl.program_id(0)
    rows = tokens.shape[0]
    flat = up.shape[0]
    rank = flat // adapters
    pieces = frozen.shape[1] // flat
    size = pieces * adapters

    @pl.when(j == 0)
    def _():
        down = maps[...]
        left[...] = wide(down).T.astype(BF)
        small[:rows, :] = (dot(tokens[...], down) * wide(slots[...])).astype(BF)
        products = dot(left[...], down)
        by_row = lax.broadcasted_iota(jnp.int32, (flat, flat), 0) // rank
        by_col = lax.broadcasted_iota(jnp.int32, (flat, flat), 1) // rank
        upper, lower = split_parts(jnp.where(by_row == by_col, products, 0.0))
        gram[:flat, :] = upper
        gram[flat:, :] = lower

    weights, outer = frozen[...], up[...]
    gram_up = dot(gram[...], outer)
    terms = wide(outer) * (2.0 * dot(left[...], weights) + gram_up[:flat] + gram_up[flat:])
    value = jnp.sum(jnp.square(wide(weights)), axis=0, keepdims=True)
    value = value + jnp.sum(terms.reshape(adapters, rank, -1), axis=1)
    value = jnp.concatenate([value[:, i * flat : (i + 1) * flat] for i in range(pieces)], axis=0)
    small[pl.ds(pl.multiple_of(rows + j * size, 16), size), :] = value.astype(BF)


def column_squares(tokens, maps, slots, frozen, up, adapters):
    rows, depth = tokens.shape
    flat, cols = up.shape

    def whole(values):
        return pl.BlockSpec(values.shape, lambda j: (0, 0))

    def moving(height):
        return pl.BlockSpec((height, SPAN), lambda j: (0, j))

    shape = (rows + cols * adapters // flat, flat)
    return pl.pallas_call(
        functools.partial(squares_kernel, adapters),
        grid=(cols // SPAN,),
        in_specs=[whole(tokens), whole(maps), whole(slots), moving(depth), moving(flat)],
        out_specs=pl.BlockSpec(shape, lambda j: (0, 0)),
        out_shape=jax.ShapeDtypeStruct(shape, BF),
        scratch_shapes=[pltpu.VMEM((flat, depth), BF), pltpu.VMEM((2 * flat, flat), BF)],
        name="squares",
        **limits(2 * flat * depth * cols, 2 * cols * depth),
    )(tokens, maps, slots, frozen, up)


def place(at, parts, height, out_shape, onto=None, after=(), begin=0):
    flat = [values for part in parts for values in part]
    count = len(flat) // len(parts)

    def kernel(at, *refs):
        out, sems = refs[-2:]
        width = out.shape[1] // len(STREAMS)
        copies = []
        for s in range(len(parts)):
            for values in refs[s * count : (s + 1) * count]:
                for first in range(0, values.shape[0], height):
                    spot = pl.multiple_of(at[len(copies)] * height, height)
                    copies.append(
                        pltpu.make_async_copy(
                            values.at[pl.ds(first, height), :],
                            out.at[pl.ds(spot, height), pl.ds((begin + s) * width, width)],
                            sems.at[len(copies)],
                        )
                    )
        for copy in copies:
            copy.start()
        for copy in copies:
            copy.wait()

    anywhere = pl.BlockSpec(memory_space=pl.ANY)
    more = list(after) + ([onto] if onto is not None else [])
    return pl.pallas_call(
        kernel,
        in_specs=[pl.BlockSpec(memory_space=pltpu.SMEM)]
        + [pl.BlockSpec(memory_space=pltpu.VMEM)] * len(flat)
        + [anywhere] * len(more),
        out_specs=anywhere,
        out_shape=out_shape,
        scratch_shapes=[pltpu.SemaphoreType.DMA((2 * len(parts),))],
        input_output_aliases={1 + len(flat) + len(after): 0} if onto is not None else {},
        compiler_params=pltpu.CompilerParams(vmem_limit_bytes=12 << 20),
        name="place",
    )(at, *flat, *more)


def place_last(at, parts, height, out_shape, onto, after):
    flat = [values for part in parts for values in part]
    count = len(flat) // len(parts)

    def kernel(at, *refs):
        out, held, sems = refs[-3:]
        width = out.shape[1] // len(STREAMS)
        loads, stores = [], []
        for s in range(len(parts)):
            for values in refs[s * count : (s + 1) * count]:
                for first in range(0, values.shape[0], height):
                    n = len(stores)
                    spot = pl.multiple_of(at[n] * height, height)
                    loads.append(
                        pltpu.make_async_copy(
                            values.at[pl.ds(first, height), :], held.at[n], sems.at[0, n]
                        )
                    )
                    stores.append(
                        pltpu.make_async_copy(
                            held.at[n],
                            out.at[pl.ds(spot, height), pl.ds(s * width, width)],
                            sems.at[1, n],
                        )
                    )
        for load in loads:
            load.start()
        for load, store in zip(loads, stores, strict=True):
            load.wait()
            store.start()
        for store in stores:
            store.wait()

    anywhere = pl.BlockSpec(memory_space=pl.ANY)
    more = [*after, onto]
    return pl.pallas_call(
        kernel,
        in_specs=[pl.BlockSpec(memory_space=pltpu.SMEM)]
        + [anywhere] * (len(flat) + len(more)),
        out_specs=anywhere,
        out_shape=out_shape,
        scratch_shapes=[
            pltpu.VMEM((2 * len(parts), height, flat[0].shape[1]), BF),
            pltpu.SemaphoreType.DMA((2, 2 * len(parts))),
        ],
        input_output_aliases={1 + len(flat) + len(after): 0},
        compiler_params=pltpu.CompilerParams(vmem_limit_bytes=12 << 20),
        name="place_last",
    )(at, *flat, *more)


def table_kernel(rows, mine, got, magnitude, table, norm, down):
    adapters, cols = magnitude.shape
    flat = mine.shape[1]
    total = wide(mine[...]) + wide(got[...])
    down[...] = total[:rows].astype(BF)
    for i in range(cols // flat):
        first = i * flat
        here = jnp.sqrt(total[rows + i * adapters : rows + (i + 1) * adapters] + 1e-06)
        norm[:, first : first + flat] = here
        scale = magnitude[:, first : first + flat] / here
        for part in range(3):
            taken = wide(scale.astype(BF))
            scale = scale - taken
            padded = jnp.concatenate([taken, jnp.zeros_like(taken)], axis=0)
            table[16 * part : 16 * part + 16, first : first + flat] = padded.astype(BF)


def grad_up_kernel(at, grad, table, hot, down, out):
    scaled = (wide(grad[...]) * dot(hot[...], table[...])).astype(BF)
    out[...] = dot(down[...], scaled, FIRST)


def grad_up_part(at, grad, table, hot, down, share):
    flat = down.shape[1]

    def mine(values):
        return pl.BlockSpec((values.shape[0], share), lambda j, at: (0, at[2]))

    def whole(values):
        return pl.BlockSpec(values.shape, lambda j, at: (0, 0))

    return pl.pallas_call(
        grad_up_kernel,
        grid_spec=pltpu.PrefetchScalarGridSpec(
            num_scalar_prefetch=1,
            grid=(1,),
            in_specs=[mine(grad), mine(table), whole(hot), whole(down)],
            out_specs=pl.BlockSpec((flat, share), lambda j, at: (0, 0)),
        ),
        out_shape=jax.ShapeDtypeStruct((flat, share), F32),
        name="grad_up",
        **limits(0, 3 * grad.shape[0] * share),
    )(at, grad, table, hot, down)


def back_kernel(grad, table, hot, up, slots, tokens, maps, *rest):
    parts, (packed, low, scaled, back) = rest[:-4], rest[-4:]
    j = pl.program_id(0)
    adapters = parts[0].shape[0] // 2
    depth = tokens.shape[1]

    @pl.when(j == 0)
    def _():
        back[...] = jnp.zeros_like(back)

    scaled[...] = (wide(grad[...]) * dot(hot[...], table[...])).astype(BF)
    back[...] += dot(scaled[...], up[...], LAST)

    @pl.when(j == pl.num_programs(0) - 1)
    def _():
        upper, lower = split_parts(back[...] * wide(slots[...]))
        low[...] = dot(upper, maps[...], LAST) + dot(lower, maps[...], LAST)
        values = tokens[...]
        packed[:, :depth] = (dot(upper, values, FIRST) + dot(lower, values, FIRST)).astype(BF)
        size = packed.shape[1] - depth
        for s in range(len(STREAMS)):
            total = wide(parts[2 * s][...]) + wide(parts[2 * s + 1][...])
            for q in range(total.shape[1] // size // 2):
                first = 2 * q * size
                both = [total[:adapters, first + k * size : first + (k + 1) * size] for k in (0, 1)]
                at = (s * (total.shape[1] // size) + 2 * q) * adapters
                packed[at : at + 2 * adapters, depth:] = jnp.concatenate(both, axis=0).astype(BF)


def back_part(grad, table, hot, up, slots, tokens, maps, parts, share):
    rows, cols = grad.shape
    depth, flat = maps.shape
    tall = hot.shape[1] // 3

    def whole(shape):
        return pl.BlockSpec(shape, lambda j: (0, 0))

    def moving(values):
        return pl.BlockSpec((values.shape[0], SPAN), lambda j: (0, j))

    def foot(values):
        return pl.BlockSpec((tall, values.shape[1]), lambda j: (values.shape[0] // tall - 1, 0))

    return pl.pallas_call(
        back_kernel,
        grid=(cols // SPAN,),
        in_specs=[moving(grad), moving(table), whole(hot.shape), moving(up)]
        + [whole(values.shape) for values in (slots, tokens, maps)]
        + [foot(values) for values in parts],
        out_specs=[whole((flat, depth + share)), whole((rows, depth)), moving(grad)],
        out_shape=[
            jax.ShapeDtypeStruct((flat, depth + share), BF),
            jax.ShapeDtypeStruct((rows, depth), F32),
            jax.ShapeDtypeStruct((rows, cols), BF),
        ],
        scratch_shapes=[pltpu.VMEM((rows, flat), F32)],
        name="back",
        **limits(2 * rows * 2 * flat * cols, 2 * cols * rows),
    )(grad, table, hot, up, slots, tokens, maps, *parts)


def backward_kernel(scaled, frozen, start, out, total):
    j = pl.program_id(0)

    @pl.when(j == 0)
    def _():
        total[...] = start[...]

    total[...] += dot(scaled[...], frozen[...], LAST)

    @pl.when(j == pl.num_programs(0) - 1)
    def _():
        out[...] = total[...].astype(BF)


def backward(scaled, frozen, start):
    rows, cols = scaled.shape
    depth = frozen.shape[0]
    span = cols // 3

    def whole(shape):
        return pl.BlockSpec(shape, lambda j: (0, 0))

    def moving(values):
        return pl.BlockSpec((values.shape[0], span), lambda j: (0, j))

    return pl.pallas_call(
        backward_kernel,
        grid=(3,),
        in_specs=[moving(scaled), moving(frozen), whole(start.shape)],
        out_specs=whole(start.shape),
        out_shape=jax.ShapeDtypeStruct(start.shape, BF),
        scratch_shapes=[pltpu.VMEM((rows, depth), F32)],
        name="backward",
        **limits(2 * rows * depth * cols, 2 * cols * (depth + rows)),
    )(scaled, frozen, start)


def on_device(
    tokens, frozen, adapter_down, adapter_up, magnitude, grad_out, tenant_lengths, tenant_adapter
):
    tok_rows, depth = tokens.shape
    adapters, cols = magnitude.shape
    flat = adapter_down.shape[1]
    block = tok_rows // SIDE
    width = cols // len(STREAMS)
    spot = {axis: lax.axis_index(axis) for axis in ("dp", "z", "y")}

    spots = [spot["dp"], jnp.int32(adapters), spot["z"] * SIDE + spot["y"]]
    early, late = [], []
    for one, two, _, _ in STREAMS:
        me = spot[one[0]]
        there = me ^ one[1]
        for which in range(SIDE):
            rest = jnp.where(which == me, 0, 3 * block + 48)
            rest = jnp.where(which == there ^ two[1], 2 * block + 32, rest)
            spots.append(jnp.where(which == there, block + 16, rest))
        early += [me, there]
        late += [me ^ two[1], there ^ two[1]]
    at, early, late = (jnp.stack(v).astype(jnp.int32) for v in (spots, early, late))
    streams, hot3, slots = forward(
        at, tenant_lengths, tenant_adapter, tokens, adapter_down, frozen, adapter_up, grad_out
    )
    small = column_squares(tokens, adapter_down, slots, frozen, adapter_up, adapters)

    def exchange(values, step):
        return [swap(v, order[step]) for v, order in zip(values, STREAMS, strict=True)]

    first = exchange([away for away, _, _ in streams], 0)
    for step, pairing in enumerate((("y", 1), ("z", 1), ("y", 3), ("z", 3))):
        if step == 0:
            small, _ = lax.optimization_barrier((small, first[0]))
        got = swap(small, pairing)
        if step < 3:
            small = round_bf(wide(small) + wide(got))
    table, col_norm, down = pl.pallas_call(
        functools.partial(table_kernel, tok_rows),
        out_shape=[
            jax.ShapeDtypeStruct((48, cols), BF),
            jax.ShapeDtypeStruct((adapters, cols), F32),
            jax.ShapeDtypeStruct((tok_rows, flat), BF),
        ],
        name="table",
        compiler_params=pltpu.CompilerParams(vmem_limit_bytes=12 << 20),
    )(small, got, magnitude)

    tall = hot3.shape[1] // 3
    sums = [
        round_bf(wide(high) + wide(got[block:]))
        for (_, high, _), got in zip(streams, first, strict=True)
    ]
    second = exchange(sums, 1)
    sums = [
        round_bf(
            jnp.concatenate(
                [
                    wide(near[:block]) + wide(got[:block]) + wide(more[tall:]),
                    wide(summed[:tall]) + wide(more[:tall]),
                ],
                axis=0,
            )
        )
        for (_, _, near), got, summed, more in zip(streams, first, sums, second, strict=True)
    ]
    got = exchange(sums, 2)
    sums = [round_bf(wide(a) + wide(b)) for a, b in zip(sums, got, strict=True)]
    got = exchange(sums, 3)

    grad_up = grad_up_part(at, grad_out, table, hot3, down, cols // SIDE**2)
    for flip in (1, 3):
        grad_up = grad_up + swap(grad_up, ("dp", flip))
    share = round_bf(grad_up)

    done = []
    for s, (a, b) in enumerate(zip(sums, got, strict=True)):
        me = spot[STREAMS[s][0][0]]
        rows = lax.dynamic_slice_in_dim(hot3, me * block, block, 0)
        scale = dot(rows, table[:, s * width : (s + 1) * width])
        done.append((scale * (wide(a[:block]) + wide(b[:block]))).astype(BF))
    near = exchange(done, 0)
    parts = [v for both in zip(sums, got, strict=True) for v in both]
    packed, low, scaled = back_part(
        grad_out, table, hot3, adapter_up, slots, tokens, adapter_down, parts, cols // SIDE**2
    )
    near, packed, low = lax.optimization_barrier((near, packed, low))
    packed = round_bf(wide(packed) + wide(swap(packed, ("dp", 1))))
    low, packed = lax.optimization_barrier((low, packed))
    pairs = [jnp.concatenate(both, axis=0) for both in zip(done, near, strict=True)]
    far = exchange(pairs, 1)
    grad_up = lax.all_gather(share, ("z", "y"), axis=1, tiled=True).astype(F32)
    packed = wide(packed) + wide(swap(packed, ("dp", 3)))
    mag = packed[:, depth:].reshape(-1, adapters, packed.shape[1] - depth)
    mag = mag.transpose(1, 0, 2).reshape(adapters, cols)
    sent = backward(scaled, frozen, low)
    sent = jnp.concatenate([sent, round_bf(packed[:, :depth])] * 2, axis=0)
    both = wide(lax.all_to_all(sent, "col", 0, 0, tiled=True))
    total = both[: tok_rows + flat] + both[tok_rows + flat :]
    input_grad = total[:tok_rows].astype(BF)
    grad_down = total[tok_rows:]
    whole = jax.ShapeDtypeStruct((tok_rows, cols), BF)
    adapted = place(early, list(zip(done, near, strict=True)), block, whole)
    after = (grad_up, input_grad)
    adapted = place_last(late, [[v] for v in far], block, whole, adapted, after)
    return (adapted, input_grad, grad_down.T, grad_up, mag / col_norm)


def solution(mesh):
    assert mesh.axis_names == ("dp", "row", "col")
    grid = Mesh(mesh.devices.reshape(SIDE, SIDE, SIDE, 2), ("dp", "z", "y", "col"))
    row = ("z", "y")
    placed = (
        P("dp", row),
        P(row, "col"),
        P(row, None),
        P(None, "col"),
        P(None, "col"),
        P("dp", "col"),
        P(),
        P(),
    )
    return jax.shard_map(
        on_device,
        mesh=grid,
        in_specs=placed,
        out_specs=(P("dp", "col"), P("dp", row), P(row, None), P(None, "col"), P(None, "col")),
        check_vma=False,
    )
```

```python
import functools

import jax
import jax.numpy as jnp
from jax import lax
from jax.experimental import pallas as pl
from jax.experimental.pallas import tpu as pltpu
from jax.sharding import Mesh
from jax.sharding import PartitionSpec as P

BF = jnp.bfloat16
F32 = jnp.float32
SIDE = 4
PLAIN = (((1,), (0,)), ((), ()))
FIRST = (((0,), (0,)), ((), ()))
LAST = (((1,), (1,)), ((), ()))

STREAMS = (
    (("y", 1), ("y", 3), ("z", 1), ("z", 3)),
    (("y", 3), ("y", 1), ("z", 3), ("z", 1)),
    (("z", 1), ("z", 3), ("y", 1), ("y", 3)),
    (("z", 3), ("z", 1), ("y", 3), ("y", 1)),
)
SPAN = 1536


def swap(values, pairing):
    axis, flip = pairing
    return lax.ppermute(values, axis, [(i, i ^ flip) for i in range(SIDE)])


def wide(values):
    return values.astype(F32)


def dot(a, b, dims=PLAIN):
    return lax.dot_general(a, b, dims, preferred_element_type=F32)


def split_parts(values):
    upper = values.astype(BF)
    return upper, (values - wide(upper)).astype(BF)


def round_bf(values):
    return lax.reduce_precision(values, exponent_bits=8, mantissa_bits=7).astype(BF)


def limits(flops, bytes_accessed):
    return dict(
        compiler_params=pltpu.CompilerParams(vmem_limit_bytes=56 << 20),
        cost_estimate=pl.CostEstimate(
            flops=flops, bytes_accessed=bytes_accessed, transcendentals=0
        ),
    )


def forward_kernel(at, lengths, owners, tokens, maps, frozen, up, grad, *rest):
    n = len(STREAMS)
    outs = [rest[3 * s : 3 * s + 3] for s in range(n)]
    hot3, slots, low, hot, stage, sems = rest[3 * n :]
    j = pl.program_id(0)
    rows = tokens.shape[0]
    block = rows // SIDE

    @pl.when(j == 0)
    def _():
        flat = slots.shape[1]
        first = at[0] * rows
        down = first + lax.broadcasted_iota(jnp.int32, slots.shape, 0)
        along = first + lax.broadcasted_iota(jnp.int32, hot.shape, 1)
        by_row, by_col = jnp.zeros_like(down), jnp.zeros_like(along)
        begin = jnp.int32(0)
        for tenant in range(lengths.shape[0]):
            by_row = jnp.where(down >= begin, owners[tenant], by_row)
            by_col = jnp.where(along >= begin, owners[tenant], by_col)
            begin = begin + lengths[tenant]
        column = lax.broadcasted_iota(jnp.int32, slots.shape, 1)
        held = jnp.where(by_row == column // (flat // at[1]), 1.0, 0.0)
        slots[...] = held.astype(BF)
        same = by_row[:, : hot3.shape[1]] == column[:, : hot3.shape[1]] % hot.shape[0]
        hot3[...] = jnp.where(same, 1.0, 0.0).astype(BF)
        same = by_col == lax.broadcasted_iota(jnp.int32, hot.shape, 0)
        hot[...] = jnp.where(same, 1.0, 0.0).astype(BF)
        low[...] = (dot(tokens[...], maps[...]) * held).astype(BF)

    total = dot(tokens[...], frozen[...]) + dot(low[...], up[...])
    mag = dot(hot[...], (total * wide(grad[...])).astype(BF)).astype(BF)
    tall = mag.shape[0]

    def copies(s):
        first = 0
        for part, out in enumerate((outs[s][2], outs[s][0], outs[s][1])):
            height = out.shape[0]
            held = stage.at[s % 2, pl.ds(first, height), :]
            yield pltpu.make_async_copy(held, out, sems.at[s % 2, part])
            first += height

    for s in range(n):

        @pl.when(j == s)
        def _(s=s):
            if s >= 2:
                for copy in copies(s - 2):
                    copy.wait()
            for first in (block, 2 * block + tall, 3 * block + 2 * tall):
                stage[s % 2, first : first + tall, :] = mag
            for which in range(SIDE):
                spot = pl.multiple_of(at[3 + SIDE * s + which], 16)
                rows_of = total[which * block : (which + 1) * block]
                stage[s % 2, pl.ds(spot, block), :] = rows_of.astype(BF)
            for copy in copies(s):
                copy.start()
            if s == n - 1:
                for copy in (*copies(s - 1), *copies(s)):
                    copy.wait()


def forward(at, lengths, owners, tokens, maps, frozen, up, grad):
    rows, depth = tokens.shape
    flat, cols = up.shape
    block = rows // SIDE
    width = cols // len(STREAMS)
    tall = 16

    def whole(shape):
        return pl.BlockSpec(shape, lambda j, *_: (0, 0))

    def moving(height):
        return pl.BlockSpec((height, width), lambda j, *_: (0, j))

    heights = (2 * block + tall, block + tall, block + tall) * len(STREAMS)
    shapes = [(height, width) for height in heights] + [(rows, 3 * tall), (rows, flat)]
    found = pl.pallas_call(
        forward_kernel,
        grid_spec=pltpu.PrefetchScalarGridSpec(
            num_scalar_prefetch=3,
            grid=(len(STREAMS),),
            in_specs=[
                whole((rows, depth)),
                whole((depth, flat)),
                moving(depth),
                moving(flat),
                moving(rows),
            ],
            out_specs=[pl.BlockSpec(memory_space=pl.ANY)] * len(heights)
            + [whole(shape) for shape in shapes[len(heights) :]],
            scratch_shapes=[
                pltpu.VMEM((rows, flat), BF),
                pltpu.VMEM((tall, rows), BF),
                pltpu.VMEM((2, rows + 3 * tall, width), BF),
                pltpu.SemaphoreType.DMA((2, 3)),
            ],
        ),
        out_shape=[jax.ShapeDtypeStruct(shape, BF) for shape in shapes],
        name="forward",
        **limits(2 * rows * (depth + 2 * flat) * cols, 2 * cols * (depth + 2 * rows)),
    )(at, lengths, owners, tokens, maps, frozen, up, grad)
    return [found[3 * s : 3 * s + 3] for s in range(len(STREAMS))], found[-2], found[-1]


def squares_kernel(adapters, tokens, maps, slots, frozen, up, small, left, gram):
    j = pl.program_id(0)
    rows = tokens.shape[0]
    flat = up.shape[0]
    rank = flat // adapters
    pieces = frozen.shape[1] // flat
    size = pieces * adapters

    @pl.when(j == 0)
    def _():
        down = maps[...]
        left[...] = wide(down).T.astype(BF)
        small[:rows, :] = (dot(tokens[...], down) * wide(slots[...])).astype(BF)
        products = dot(left[...], down)
        by_row = lax.broadcasted_iota(jnp.int32, (flat, flat), 0) // rank
        by_col = lax.broadcasted_iota(jnp.int32, (flat, flat), 1) // rank
        upper, lower = split_parts(jnp.where(by_row == by_col, products, 0.0))
        gram[:flat, :] = upper
        gram[flat:, :] = lower

    weights, outer = frozen[...], up[...]
    gram_up = dot(gram[...], outer)
    terms = wide(outer) * (2.0 * dot(left[...], weights) + gram_up[:flat] + gram_up[flat:])
    value = jnp.sum(jnp.square(wide(weights)), axis=0, keepdims=True)
    value = value + jnp.sum(terms.reshape(adapters, rank, -1), axis=1)
    value = jnp.concatenate([value[:, i * flat : (i + 1) * flat] for i in range(pieces)], axis=0)
    small[pl.ds(pl.multiple_of(rows + j * size, 16), size), :] = value.astype(BF)


def column_squares(tokens, maps, slots, frozen, up, adapters):
    rows, depth = tokens.shape
    flat, cols = up.shape

    def whole(values):
        return pl.BlockSpec(values.shape, lambda j: (0, 0))

    def moving(height):
        return pl.BlockSpec((height, SPAN), lambda j: (0, j))

    shape = (rows + cols * adapters // flat, flat)
    return pl.pallas_call(
        functools.partial(squares_kernel, adapters),
        grid=(cols // SPAN,),
        in_specs=[whole(tokens), whole(maps), whole(slots), moving(depth), moving(flat)],
        out_specs=pl.BlockSpec(shape, lambda j: (0, 0)),
        out_shape=jax.ShapeDtypeStruct(shape, BF),
        scratch_shapes=[pltpu.VMEM((flat, depth), BF), pltpu.VMEM((2 * flat, flat), BF)],
        name="squares",
        **limits(2 * flat * depth * cols, 2 * cols * depth),
    )(tokens, maps, slots, frozen, up)


def place(at, parts, height, out_shape, onto=None, after=(), begin=0):
    flat = [values for part in parts for values in part]
    count = len(flat) // len(parts)

    def kernel(at, *refs):
        out, sems = refs[-2:]
        width = out.shape[1] // len(STREAMS)
        copies = []
        for s in range(len(parts)):
            for values in refs[s * count : (s + 1) * count]:
                for first in range(0, values.shape[0], height):
                    spot = pl.multiple_of(at[len(copies)] * height, height)
                    copies.append(
                        pltpu.make_async_copy(
                            values.at[pl.ds(first, height), :],
                            out.at[pl.ds(spot, height), pl.ds((begin + s) * width, width)],
                            sems.at[len(copies)],
                        )
                    )
        for copy in copies:
            copy.start()
        for copy in copies:
            copy.wait()

    anywhere = pl.BlockSpec(memory_space=pl.ANY)
    more = list(after) + ([onto] if onto is not None else [])
    return pl.pallas_call(
        kernel,
        in_specs=[pl.BlockSpec(memory_space=pltpu.SMEM)]
        + [pl.BlockSpec(memory_space=pltpu.VMEM)] * len(flat)
        + [anywhere] * len(more),
        out_specs=anywhere,
        out_shape=out_shape,
        scratch_shapes=[pltpu.SemaphoreType.DMA((2 * len(parts),))],
        input_output_aliases={1 + len(flat) + len(after): 0} if onto is not None else {},
        compiler_params=pltpu.CompilerParams(vmem_limit_bytes=12 << 20),
        name="place",
    )(at, *flat, *more)


def place_last(at, parts, height, out_shape, onto, after):
    flat = [values for part in parts for values in part]
    count = len(flat) // len(parts)

    def kernel(at, *refs):
        out, held, sems = refs[-3:]
        width = out.shape[1] // len(STREAMS)
        loads, stores = [], []
        for s in range(len(parts)):
            for values in refs[s * count : (s + 1) * count]:
                for first in range(0, values.shape[0], height):
                    n = len(stores)
                    spot = pl.multiple_of(at[n] * height, height)
                    loads.append(
                        pltpu.make_async_copy(
                            values.at[pl.ds(first, height), :], held.at[n], sems.at[0, n]
                        )
                    )
                    stores.append(
                        pltpu.make_async_copy(
                            held.at[n],
                            out.at[pl.ds(spot, height), pl.ds(s * width, width)],
                            sems.at[1, n],
                        )
                    )
        for load in loads:
            load.start()
        for load, store in zip(loads, stores, strict=True):
            load.wait()
            store.start()
        for store in stores:
            store.wait()

    anywhere = pl.BlockSpec(memory_space=pl.ANY)
    more = [*after, onto]
    return pl.pallas_call(
        kernel,
        in_specs=[pl.BlockSpec(memory_space=pltpu.SMEM)]
        + [anywhere] * (len(flat) + len(more)),
        out_specs=anywhere,
        out_shape=out_shape,
        scratch_shapes=[
            pltpu.VMEM((2 * len(parts), height, flat[0].shape[1]), BF),
            pltpu.SemaphoreType.DMA((2, 2 * len(parts))),
        ],
        input_output_aliases={1 + len(flat) + len(after): 0},
        compiler_params=pltpu.CompilerParams(vmem_limit_bytes=12 << 20),
        name="place_last",
    )(at, *flat, *more)


def table_kernel(rows, mine, got, magnitude, table, norm, down):
    adapters, cols = magnitude.shape
    flat = mine.shape[1]
    total = wide(mine[...]) + wide(got[...])
    down[...] = total[:rows].astype(BF)
    for i in range(cols // flat):
        first = i * flat
        here = jnp.sqrt(total[rows + i * adapters : rows + (i + 1) * adapters] + 1e-06)
        norm[:, first : first + flat] = here
        scale = magnitude[:, first : first + flat] / here
        for part in range(3):
            taken = wide(scale.astype(BF))
            scale = scale - taken
            padded = jnp.concatenate([taken, jnp.zeros_like(taken)], axis=0)
            table[16 * part : 16 * part + 16, first : first + flat] = padded.astype(BF)


def grad_up_kernel(at, grad, table, hot, down, out):
    scaled = (wide(grad[...]) * dot(hot[...], table[...])).astype(BF)
    out[...] = dot(down[...], scaled, FIRST).astype(BF)


def grad_up_part(at, grad, table, hot, down, share):
    flat = down.shape[1]

    def mine(values):
        return pl.BlockSpec((values.shape[0], share), lambda j, at: (0, at[2]))

    def whole(values):
        return pl.BlockSpec(values.shape, lambda j, at: (0, 0))

    return pl.pallas_call(
        grad_up_kernel,
        grid_spec=pltpu.PrefetchScalarGridSpec(
            num_scalar_prefetch=1,
            grid=(1,),
            in_specs=[mine(grad), mine(table), whole(hot), whole(down)],
            out_specs=pl.BlockSpec((flat, share), lambda j, at: (0, 0)),
        ),
        out_shape=jax.ShapeDtypeStruct((flat, share), BF),
        name="grad_up",
        **limits(0, 3 * grad.shape[0] * share),
    )(at, grad, table, hot, down)


def back_kernel(grad, table, hot, up, slots, tokens, maps, *rest):
    parts, (packed, low, scaled, back) = rest[:-4], rest[-4:]
    j = pl.program_id(0)
    adapters = parts[0].shape[0] // 2
    depth = tokens.shape[1]

    @pl.when(j == 0)
    def _():
        back[...] = jnp.zeros_like(back)

    scaled[...] = (wide(grad[...]) * dot(hot[...], table[...])).astype(BF)
    back[...] += dot(scaled[...], up[...], LAST)

    @pl.when(j == pl.num_programs(0) - 1)
    def _():
        upper, lower = split_parts(back[...] * wide(slots[...]))
        low[...] = dot(upper, maps[...], LAST) + dot(lower, maps[...], LAST)
        values = tokens[...]
        packed[:, :depth] = (dot(upper, values, FIRST) + dot(lower, values, FIRST)).astype(BF)
        size = packed.shape[1] - depth
        for s in range(len(STREAMS)):
            total = wide(parts[2 * s][...]) + wide(parts[2 * s + 1][...])
            for q in range(total.shape[1] // size // 2):
                first = 2 * q * size
                both = [total[:adapters, first + k * size : first + (k + 1) * size] for k in (0, 1)]
                at = (s * (total.shape[1] // size) + 2 * q) * adapters
                packed[at : at + 2 * adapters, depth:] = jnp.concatenate(both, axis=0).astype(BF)


def back_part(grad, table, hot, up, slots, tokens, maps, parts, share):
    rows, cols = grad.shape
    depth, flat = maps.shape
    tall = hot.shape[1] // 3

    def whole(shape):
        return pl.BlockSpec(shape, lambda j: (0, 0))

    def moving(values):
        return pl.BlockSpec((values.shape[0], SPAN), lambda j: (0, j))

    def foot(values):
        return pl.BlockSpec((tall, values.shape[1]), lambda j: (values.shape[0] // tall - 1, 0))

    return pl.pallas_call(
        back_kernel,
        grid=(cols // SPAN,),
        in_specs=[moving(grad), moving(table), whole(hot.shape), moving(up)]
        + [whole(values.shape) for values in (slots, tokens, maps)]
        + [foot(values) for values in parts],
        out_specs=[whole((flat, depth + share)), whole((rows, depth)), moving(grad)],
        out_shape=[
            jax.ShapeDtypeStruct((flat, depth + share), BF),
            jax.ShapeDtypeStruct((rows, depth), F32),
            jax.ShapeDtypeStruct((rows, cols), BF),
        ],
        scratch_shapes=[pltpu.VMEM((rows, flat), F32)],
        name="back",
        **limits(2 * rows * 2 * flat * cols, 2 * cols * rows),
    )(grad, table, hot, up, slots, tokens, maps, *parts)


def backward_kernel(scaled, frozen, start, out, total):
    j = pl.program_id(0)

    @pl.when(j == 0)
    def _():
        total[...] = start[...]

    total[...] += dot(scaled[...], frozen[...], LAST)

    @pl.when(j == pl.num_programs(0) - 1)
    def _():
        out[...] = total[...].astype(BF)


def backward(scaled, frozen, start):
    rows, cols = scaled.shape
    depth = frozen.shape[0]
    span = cols // 3

    def whole(shape):
        return pl.BlockSpec(shape, lambda j: (0, 0))

    def moving(values):
        return pl.BlockSpec((values.shape[0], span), lambda j: (0, j))

    return pl.pallas_call(
        backward_kernel,
        grid=(3,),
        in_specs=[moving(scaled), moving(frozen), whole(start.shape)],
        out_specs=whole(start.shape),
        out_shape=jax.ShapeDtypeStruct(start.shape, BF),
        scratch_shapes=[pltpu.VMEM((rows, depth), F32)],
        name="backward",
        **limits(2 * rows * depth * cols, 2 * cols * (depth + rows)),
    )(scaled, frozen, start)


def on_device(
    tokens, frozen, adapter_down, adapter_up, magnitude, grad_out, tenant_lengths, tenant_adapter
):
    tok_rows, depth = tokens.shape
    adapters, cols = magnitude.shape
    flat = adapter_down.shape[1]
    block = tok_rows // SIDE
    width = cols // len(STREAMS)
    spot = {axis: lax.axis_index(axis) for axis in ("dp", "z", "y")}

    spots = [spot["dp"], jnp.int32(adapters), spot["z"] * SIDE + spot["y"]]
    early, late = [], []
    for one, two, _, _ in STREAMS:
        me = spot[one[0]]
        there = me ^ one[1]
        for which in range(SIDE):
            rest = jnp.where(which == me, 0, 3 * block + 48)
            rest = jnp.where(which == there ^ two[1], 2 * block + 32, rest)
            spots.append(jnp.where(which == there, block + 16, rest))
        early += [me, there]
        late += [me ^ two[1], there ^ two[1]]
    at, early, late = (jnp.stack(v).astype(jnp.int32) for v in (spots, early, late))
    streams, hot3, slots = forward(
        at, tenant_lengths, tenant_adapter, tokens, adapter_down, frozen, adapter_up, grad_out
    )
    small = column_squares(tokens, adapter_down, slots, frozen, adapter_up, adapters)

    def exchange(values, step):
        return [swap(v, order[step]) for v, order in zip(values, STREAMS, strict=True)]

    first = exchange([away for away, _, _ in streams], 0)
    for step, pairing in enumerate((("y", 1), ("z", 1), ("y", 3), ("z", 3))):
        if step == 0:
            small, _ = lax.optimization_barrier((small, first[0]))
        got = swap(small, pairing)
        if step < 3:
            small = round_bf(wide(small) + wide(got))
    table, col_norm, down = pl.pallas_call(
        functools.partial(table_kernel, tok_rows),
        out_shape=[
            jax.ShapeDtypeStruct((48, cols), BF),
            jax.ShapeDtypeStruct((adapters, cols), F32),
            jax.ShapeDtypeStruct((tok_rows, flat), BF),
        ],
        name="table",
        compiler_params=pltpu.CompilerParams(vmem_limit_bytes=12 << 20),
    )(small, got, magnitude)

    tall = hot3.shape[1] // 3
    sums = [
        round_bf(wide(high) + wide(got[block:]))
        for (_, high, _), got in zip(streams, first, strict=True)
    ]
    second = exchange(sums, 1)
    sums = [
        round_bf(
            jnp.concatenate(
                [
                    wide(near[:block]) + wide(got[:block]) + wide(more[tall:]),
                    wide(summed[:tall]) + wide(more[:tall]),
                ],
                axis=0,
            )
        )
        for (_, _, near), got, summed, more in zip(streams, first, sums, second, strict=True)
    ]
    got = exchange(sums, 2)
    sums = [round_bf(wide(a) + wide(b)) for a, b in zip(sums, got, strict=True)]
    got = exchange(sums, 3)

    grad_up = grad_up_part(at, grad_out, table, hot3, down, cols // SIDE**2)
    share = grad_up
    for flip in (1, 3):
        share = round_bf(wide(share) + wide(swap(share, ("dp", flip))))

    done = []
    for s, (a, b) in enumerate(zip(sums, got, strict=True)):
        me = spot[STREAMS[s][0][0]]
        rows = lax.dynamic_slice_in_dim(hot3, me * block, block, 0)
        scale = dot(rows, table[:, s * width : (s + 1) * width])
        done.append((scale * (wide(a[:block]) + wide(b[:block]))).astype(BF))
    near = exchange(done, 0)
    parts = [v for both in zip(sums, got, strict=True) for v in both]
    packed, low, scaled = back_part(
        grad_out, table, hot3, adapter_up, slots, tokens, adapter_down, parts, cols // SIDE**2
    )
    near, packed, low = lax.optimization_barrier((near, packed, low))
    packed = round_bf(wide(packed) + wide(swap(packed, ("dp", 1))))
    low, packed = lax.optimization_barrier((low, packed))
    pairs = [jnp.concatenate(both, axis=0) for both in zip(done, near, strict=True)]
    far = exchange(pairs, 1)
    grad_up = lax.all_gather(share, ("z", "y"), axis=1, tiled=True).astype(F32)
    packed = wide(packed) + wide(swap(packed, ("dp", 3)))
    mag = packed[:, depth:].reshape(-1, adapters, packed.shape[1] - depth)
    mag = mag.transpose(1, 0, 2).reshape(adapters, cols)
    sent = backward(scaled, frozen, low)
    sent = jnp.concatenate([sent, round_bf(packed[:, :depth])] * 2, axis=0)
    both = wide(lax.all_to_all(sent, "col", 0, 0, tiled=True))
    total = both[: tok_rows + flat] + both[tok_rows + flat :]
    input_grad = total[:tok_rows].astype(BF)
    grad_down = total[tok_rows:]
    whole = jax.ShapeDtypeStruct((tok_rows, cols), BF)
    adapted = place(early, list(zip(done, near, strict=True)), block, whole)
    after = (grad_up,)
    adapted = place_last(late, [[v] for v in far], block, whole, adapted, after)
    return (adapted, input_grad, grad_down.T, grad_up, mag / col_norm)


def solution(mesh):
    assert mesh.axis_names == ("dp", "row", "col")
    grid = Mesh(mesh.devices.reshape(SIDE, SIDE, SIDE, 2), ("dp", "z", "y", "col"))
    row = ("z", "y")
    placed = (
        P("dp", row),
        P(row, "col"),
        P(row, None),
        P(None, "col"),
        P(None, "col"),
        P("dp", "col"),
        P(),
        P(),
    )
    return jax.shard_map(
        on_device,
        mesh=grid,
        in_specs=placed,
        out_specs=(P("dp", "col"), P("dp", row), P(row, None), P(None, "col"), P(None, "col")),
        check_vma=False,
    )
```
